256 devices in a mesh: sect: 64 (over x, z, core), blk: 4 (over y).
Axes of the slice: x: 4, y: 4, z: 8, core: 2. Of those that a mesh axis runs over, the one named last changes fastest.
Arguments:
- psi_guess: bfloat16 [64, 32, 128, 128], P('sect', 'blk'), may hold values from -6 to 6
- sector_sizes: int32 [64, 32], P('sect'), may hold values from 1 to 128, 2048 in all within a row
- slot_sector: int32 [32], replicated, may hold values from 0 to 31, each once
- pair_table: int32 [32, 16], replicated, may hold values from 0 to 31
- left_ops: bfloat16 [64, 32, 16, 128, 128], P('sect', 'blk'), may hold values from -0.5 to 0.5
- right_ops: bfloat16 [64, 32, 16, 128, 128], P('sect', 'blk'), may hold values from -0.5 to 0.5
- decay: float32 [64, 32, 128], P('sect', 'blk'), may hold values from 0.9 to 0.999
- source_h: float32 [64, 32, 128, 128], P('sect', 'blk'), may hold values from -1 to 1
- precond: float32 [64, 32, 128, 128], P('sect', 'blk'), may hold values from 1 to 10
- inv_sv: float32 [64, 32, 128], P('sect', 'blk'), may hold values from 1 to 10
- ranks: int32 [64, 32], P('sect'), may hold values from 1 to 128
Outputs:
- ground: bfloat16 [64, 32, 128, 128], P('sect', 'blk')
- energies: float32 [64], P('sect')
- merged: bfloat16 [64, 32, 128, 128], P('sect', 'blk')
The draws below stay inside these ranges and needn't reach their ends.
Inputs may be any that keep to these rules, and one draw needn't show every extreme that they name: `slot_sector`: each sector appears in exactly one slot. `sector_sizes`: each row sums to 2048.
All inputs are finite; a program needn't handle non-finite values.
Results may differ from the reference program's by a relative error of at most 0.02.
Values may be sent and summed in bfloat16 or wider, within the bound.
No kernel may reach another device: no remote copies, remote signals or barrier semaphores. Data moves between devices by JAX's collectives and lax.ppermute only.
A program may use at most 128 MiB of HBM per device.

```python
import math
import jax
import jax.numpy as jnp
import numpy as np
from jax import lax

M = 2048
CAP = 128
W = 16
STEPS = 3
NSEC = 32
SECTIONS = 64


def touch_ends(array, key, smallest, high):
    shape = array.shape
    place = [jax.random.randint(jax.random.fold_in(key, axis), (), 0, shape[axis]) for axis in range(len(shape))]
    array = array.at[tuple(place)].set(smallest)
    longest = shape.index(max(shape))
    place[longest] = (place[longest] + 1) % shape[longest]
    return array.at[tuple(place)].set(high)


def block_levels(rng, extent, shards, least, top_value):
    loudness = 1.0
    for axis_at, shards_of in shards:
        heights = jax.random.uniform(jax.random.fold_in(jax.random.fold_in(rng, 6), axis_at), (shards_of,), jnp.float32, least / len(shards), top_value / len(shards))
        loudness = loudness * jnp.repeat(jnp.exp(heights), extent[axis_at] // shards_of).reshape((-1,) + (1,) * (len(extent) - 1 - axis_at))
    return loudness


def split_up(amount, total, most, slope):
    weights = [(1 << 20) // math.isqrt(rank ** slope) + 1 for rank in range(2, amount + 1)]
    spare, holding = total - most - (amount - 1), [1] * (amount - 1)
    while spare > 0:
        candidates = [i for i in range(amount - 1) if holding[i] < most]
        mass, remaining = sum([weights[i] for i in candidates]), spare
        for i in candidates:
            extra = min(most - holding[i], max(1, remaining * weights[i] // mass), spare)
            holding[i] = holding[i] + extra
            spare = spare - extra
    return np.array([most] + holding)


def ragged(stream_key, number_of, total, most, skew):
    if number_of == 2:
        one = jax.random.randint(stream_key, (), max(1, total - most), min(most, total - 1) + 1)
        return jnp.stack([one, total - one])
    tallies = jnp.asarray(split_up(number_of, total, most, skew), jnp.int32)
    pairs = (number_of - 1) // 2
    source_of, sink = tallies[1:1 + 2 * pairs:2], tallies[2:2 + 2 * pairs:2]
    margin = jnp.minimum(source_of - 1, most - sink)
    passed = jax.random.randint(jax.random.fold_in(stream_key, 1), (pairs,), 0, 1 << 20) % (margin + 1)
    tallies = tallies.at[1:1 + 2 * pairs:2].set(source_of - passed).at[2:2 + 2 * pairs:2].set(sink + passed)
    return tallies[jax.random.permutation(jax.random.fold_in(stream_key, 2), number_of)]


def bell_draw(rng, extent, width, reach, split=(), kind=jnp.bfloat16):
    factor_of = block_levels(rng, extent, split, -0.22, 0.18) if split else 1.0
    result = jax.random.normal(rng, extent, jnp.float32) * width * factor_of
    return jnp.minimum(jnp.maximum(result, -reach), reach).astype(kind)


def setup_inputs(seed: int = 0) -> dict:
    streams_of = jax.random.split(jax.random.key(seed), 12)
    return {
        "psi_guess": bell_draw(streams_of[0], (SECTIONS, NSEC, CAP, CAP), 1.0, 6.0, ((0, 64), (1, 4))),
        "sector_sizes": jax.vmap(lambda own: ragged(own, NSEC, M, CAP, 2))(jax.random.split(streams_of[1], SECTIONS)).reshape((SECTIONS, NSEC)).astype(jnp.int32),
        "slot_sector": jax.random.permutation(streams_of[2], NSEC).astype(jnp.int32),
        "pair_table": touch_ends(jax.random.randint(streams_of[3], (NSEC, W), 0, NSEC), jax.random.fold_in(streams_of[3], 1), 0, NSEC - 1).astype(jnp.int32),
        "left_ops": bell_draw(streams_of[4], (SECTIONS, NSEC, W, CAP, CAP), CAP ** -0.5, 0.5, ((0, 64), (1, 4))),
        "right_ops": bell_draw(streams_of[5], (SECTIONS, NSEC, W, CAP, CAP), CAP ** -0.5, 0.5, ((0, 64), (1, 4))),
        "decay": jnp.clip(jnp.exp(math.log(0.999) - 0.10436005 * jax.random.uniform(streams_of[6], (SECTIONS, NSEC, CAP), jnp.float32) ** block_levels(streams_of[6], (SECTIONS, NSEC, CAP), ((0, 64), (1, 4)), -0.2, 0.2)), 0.9, 0.999),
        "source_h": bell_draw(streams_of[7], (SECTIONS, NSEC, CAP, CAP), 0.125, 1.0, ((0, 64), (1, 4)), jnp.float32),
        "precond": jnp.clip(jnp.exp(math.log(10.0) - 2.3025851 * jax.random.uniform(streams_of[8], (SECTIONS, NSEC, CAP, CAP), jnp.float32) ** block_levels(streams_of[8], (SECTIONS, NSEC, CAP, CAP), ((0, 64), (1, 4)), -0.2, 0.2)), 1.0, 10.0),
        "inv_sv": jnp.clip(jnp.exp(math.log(10.0) - 2.3025851 * jax.random.uniform(streams_of[9], (SECTIONS, NSEC, CAP), jnp.float32) ** block_levels(streams_of[9], (SECTIONS, NSEC, CAP), ((0, 64), (1, 4)), -0.2, 0.2)), 1.0, 10.0),
        "ranks": touch_ends(jax.random.randint(streams_of[10], (SECTIONS, NSEC), 1, CAP + 1), jax.random.fold_in(streams_of[10], 1), 1, CAP).astype(jnp.int32),
    }


damping = 0.5

def reference(psi_guess, sector_sizes, slot_sector, pair_table, left_ops, right_ops, decay, source_h, precond, inv_sv, ranks):
    positions = jnp.arange(CAP, dtype=jnp.int32)
    sector_ids = jnp.arange(NSEC, dtype=jnp.int32)
    sizes_slot = sector_sizes[:, slot_sector]
    ranks_slot = ranks[:, slot_sector]
    inside = positions[None, None, :] < sizes_slot[:, :, None]
    support = (inside[:, :, :, None] & inside[:, :, None, :]).astype(jnp.float32)
    psi_start = (psi_guess.astype(jnp.float32) * support).astype(jnp.bfloat16)

    def advance(carried, inputs):
        factor, source = inputs
        return (factor[:, :, None] * carried * factor[:, None, :] + source, carried)
    final_env, environment = lax.scan(advance, jnp.zeros((NSEC, CAP, CAP), jnp.float32), (decay, source_h))
    env_low = environment.astype(jnp.bfloat16)
    slot_of = lax.optimization_barrier(jnp.sum(jnp.where(slot_sector[:, None] == sector_ids[None, :], sector_ids[:, None], 0), axis=0)).astype(jnp.int32)
    source_slot = slot_of[pair_table[slot_sector]]

    def davidson(inputs):
        psi_now, env_now, left_now, right_now, support_now, precond_now = inputs
        rayleigh = jnp.float32(0.0)
        for iteration in range(STEPS):
            sources = psi_now[source_slot]
            inner_left = jnp.einsum('jwik,jwkl->jwil', left_now.astype(jnp.float32), sources.astype(jnp.float32)).astype(jnp.bfloat16)
            operator_terms = jnp.einsum('jwil,jwml->jim', inner_left.astype(jnp.float32), right_now.astype(jnp.float32))
            env_term = jnp.einsum('jik,jkl->jil', env_now.astype(jnp.float32), psi_now.astype(jnp.float32))
            applied = (env_term + operator_terms) * support_now
            current = psi_now.astype(jnp.float32)
            rayleigh = jnp.sum(current * applied) / jnp.sum(current * current)
            updated = current - damping * (applied - rayleigh * current) / precond_now
            psi_now = (updated * lax.rsqrt(jnp.mean(updated * updated) + 1e-06)).astype(jnp.bfloat16)
        return (psi_now, rayleigh)
    ground, energies = lax.map(davidson, (psi_start, env_low, left_ops, right_ops, support, precond))
    kept_mask = (positions[None, None, :] < ranks_slot[:, :, None]).astype(jnp.float32)
    weight = inv_sv * kept_mask / CAP
    scaled = (ground.astype(jnp.float32) * weight[:, :, None, :]).astype(jnp.bfloat16)
    following = jnp.concatenate([ground[1:], jnp.zeros_like(ground[:1])], axis=0)
    merged = jnp.einsum('sjik,sjkl->sjil', scaled.astype(jnp.float32), following.astype(jnp.float32)).astype(jnp.bfloat16)
    return (ground, energies, merged)
```

```python
import functools

import jax
import jax.numpy as jnp
from jax import lax
from jax.experimental import pallas as pl
from jax.experimental.pallas import tpu as pltpu
from jax.sharding import PartitionSpec as P

STEPS = 3
DAMPING = 0.5
F32 = jnp.float32
BF16 = jnp.bfloat16
VMEM = pltpu.VMEM
SMEM = pltpu.SMEM
LIMIT = 32 * 1024 * 1024


def params(**more):
    return pltpu.CompilerParams(vmem_limit_bytes=LIMIT, **more)


def whole(space=VMEM):
    return pl.BlockSpec(memory_space=space)


def cost(flops, bytes_accessed):
    return pl.CostEstimate(flops=flops, bytes_accessed=bytes_accessed, transcendentals=0)


def start_kernel(psi_ref, precond_ref, out_ref):
    rows = psi_ref.shape[0]
    out_ref[0:rows, :] = psi_ref[...]
    out_ref[rows : 2 * rows, :] = (DAMPING / precond_ref[...]).astype(BF16)


def start_message(psi_guess, precond):
    rows, cap = psi_guess.shape
    return pl.pallas_call(
        start_kernel,
        out_shape=jax.ShapeDtypeStruct((2 * rows, cap), BF16),
        in_specs=[whole(), whole()],
        out_specs=whole(),
        compiler_params=params(),
        cost_estimate=cost(2 * rows * cap, 10 * rows * cap),
        name="start_message",
    )(psi_guess, precond)


def chip_kernel(core_ref, own_h, other_h, own_d, other_d, out_ref, late_t):
    slots, cap = own_d.shape
    chunk = out_ref.shape[1] - 16
    cuts = cap // chunk

    def emit(first_h, second_h, first_d, second_d):
        late_t[...] = jnp.transpose(second_d[...])
        total = first_d[...] * second_d[...]
        high = total.astype(BF16)
        low = (total - high.astype(F32)).astype(BF16)
        row = lax.broadcasted_iota(jnp.int32, (16, cap), 0)
        for j in range(slots):
            columns = late_t[:, j : j + 1]
            both = columns * first_h[j] * second_d[j : j + 1, :] + second_h[j]
            tail = jnp.where(
                row == 0,
                high[j : j + 1, :].astype(F32),
                jnp.where(row == 1, low[j : j + 1, :].astype(F32), 0.0),
            ).astype(BF16)
            for cut in range(cuts):
                out_ref[j * cuts + cut, 0:chunk, :] = both[cut * chunk : (cut + 1) * chunk].astype(BF16)
                out_ref[j * cuts + cut, chunk : chunk + 16, :] = tail

    @pl.when(core_ref[0] == 0)
    def _():
        emit(own_h, other_h, own_d, other_d)

    @pl.when(core_ref[0] != 0)
    def _():
        emit(other_h, own_h, other_d, own_d)


def chip_maps(core, own_h, other_h, own_d, other_d, chips):
    slots, cap = own_d.shape
    chunk = slots * cap // chips
    return pl.pallas_call(
        chip_kernel,
        out_shape=jax.ShapeDtypeStruct((chips, chunk + 16, cap), BF16),
        in_specs=[whole(SMEM)] + [whole()] * 4,
        out_specs=whole(),
        scratch_shapes=[pltpu.VMEM((cap, slots), F32)],
        compiler_params=params(),
        cost_estimate=cost(4 * slots * cap * cap, 12 * slots * cap * cap),
        name="chip_maps",
    )(core, own_h, other_h, own_d, other_d)


def scan_kernel(chip_ref, maps_ref, out_ref, factor, factor_t):
    chips, chunk, cap = out_ref.shape
    cuts = cap // chunk
    for z in range(chips):
        tail = maps_ref[z, chunk : chunk + 16, :].astype(F32)
        factor[z : z + 1, :] = tail[0:1, :] + tail[1:2, :]
    factor_t[...] = jnp.transpose(factor[...])
    first = pl.multiple_of(lax.rem(chip_ref[0], cuts) * chunk, chunk)
    columns = factor_t[pl.ds(first, chunk), :]
    state = jnp.zeros((chunk, cap), F32)
    for z in range(chips):
        out_ref[z] = state.astype(BF16)
        source = maps_ref[z, 0:chunk, :].astype(F32)
        state = columns[:, z : z + 1] * state * factor[z : z + 1, :] + source


def scan_maps(chip, maps):
    chips, rows, cap = maps.shape
    chunk = rows - 16
    return pl.pallas_call(
        scan_kernel,
        out_shape=jax.ShapeDtypeStruct((chips, chunk, cap), BF16),
        in_specs=[whole(SMEM), whole()],
        out_specs=whole(),
        scratch_shapes=[pltpu.VMEM((chips, cap), F32), pltpu.VMEM((cap, chips), F32)],
        compiler_params=params(),
        cost_estimate=cost(4 * chips * chunk * cap, 5 * chips * chunk * cap),
        name="scan_maps",
    )(chip, maps)


def pack_sums(values, cap):
    row = lax.broadcasted_iota(jnp.int32, (16, cap), 0)
    tile = jnp.zeros((16, cap), F32)
    for k, value in enumerate(values):
        rest = jnp.broadcast_to(value, (16, cap))
        for piece in range(3):
            part = rest.astype(BF16).astype(F32)
            tile = jnp.where(row == 3 * k + piece, part, tile)
            rest = rest - part
    return tile.astype(BF16)


def unpack_sums(tile):
    tile = tile.astype(F32)
    return [
        tile[3 * k : 3 * k + 1] + tile[3 * k + 1 : 3 * k + 2] + tile[3 * k + 2 : 3 * k + 3]
        for k in range(5)
    ]


def local_quotient(numerator, overlap):
    return jnp.where(overlap > 0.0, numerator / jnp.where(overlap > 0.0, overlap, 1.0), 0.0)


def paired(values):
    return (values[0] + values[2]) + (values[1] + values[3])


def resolve(tiles, entries):
    sums = [unpack_sums(tile) for tile in tiles]
    rayleigh = paired([s[0] for s in sums]) / paired([s[1] for s in sums])
    deltas = [rayleigh - local_quotient(s[0], s[1]) for s in sums]
    squares = paired(
        [s[2] + delta * (2.0 * s[3] + delta * s[4]) for s, delta in zip(sums, deltas)]
    )
    scale = lax.rsqrt(squares / entries + 1e-06)
    return rayleigh, deltas, scale


def total(x):
    return jnp.sum(jnp.sum(x, axis=0, keepdims=True), axis=1, keepdims=True)


def products(j, me, slot_sector, pair_table, slot_of, left_ref, right_ref, psi_ref, inner):
    slots = psi_ref.shape[0] // 4
    terms, cap = left_ref.shape[1], left_ref.shape[2]
    sector = slot_sector[me * slots + j]
    for w in range(terms):
        source = slot_of[pair_table[sector, w]]
        owner = source // slots
        place = lax.rem(me - owner + 4, 4) * slots + lax.rem(source, slots)
        inner[:, w * cap : (w + 1) * cap] = jnp.dot(
            left_ref[0, w], psi_ref[place], preferred_element_type=F32
        ).astype(BF16)
    result = jnp.zeros((cap, cap), F32)
    for w in range(0, terms, 2):
        pair = jnp.concatenate([right_ref[0, w], right_ref[0, w + 1]], axis=1)
        result = result + lax.dot_general(
            inner[:, w * cap : (w + 2) * cap],
            pair,
            (((1,), (1,)), ((), ())),
            preferred_element_type=F32,
        )
    return result


def invert_slots(slot_sector, slot_of):
    def one(slot, carry):
        slot_of[slot_sector[slot]] = slot
        return carry

    lax.fori_loop(0, slot_sector.shape[0], one, 0)


def support_of(size, cap):
    row = lax.broadcasted_iota(jnp.int32, (cap, cap), 0)
    column = lax.broadcasted_iota(jnp.int32, (cap, cap), 1)
    return (row < size) & (column < size)


def close_step(slots, psi_ref, precond_ref, applied, a_ref, message_ref):
    cap = applied.shape[1]
    zero = jnp.zeros((cap, cap), F32)
    numerator, overlap = zero, zero
    for j in range(slots):
        current = psi_ref[j].astype(F32)
        numerator = numerator + current * applied[j]
        overlap = overlap + current * current
    numerator, overlap = total(numerator), total(overlap)
    quotient = local_quotient(numerator, overlap)
    aa, ab, bb = zero, zero, zero
    for j in range(slots):
        current = psi_ref[j].astype(F32)
        half = DAMPING / precond_ref[j]
        a = current - half * (applied[j] - quotient * current)
        b = half * current
        a_ref[j] = a
        if message_ref.shape[0] > 16:
            message_ref[j * cap : (j + 1) * cap, :] = a.astype(BF16)
        aa = aa + a * a
        ab = ab + a * b
        bb = bb + b * b
    sums = [numerator, overlap, total(aa), total(ab), total(bb)]
    rows = message_ref.shape[0]
    message_ref[rows - 16 : rows, :] = pack_sums(sums, cap)


def first_kernel(
    place_ref,
    slot_sector,
    pair_table,
    sizes,
    own_ref,
    psi_1,
    psi_2,
    psi_3,
    env_ref,
    other_h,
    other_d,
    precond_ref,
    left_ref,
    right_ref,
    psi_ref,
    env_low,
    a_ref,
    message_ref,
    applied,
    inner,
    other_t,
    slot_of,
):
    j = pl.program_id(0)
    slots, cap = applied.shape[0], applied.shape[1]
    me, core = place_ref[0], place_ref[1]

    @pl.when(j == 0)
    def _():
        invert_slots(slot_sector, slot_of)
        other_t[...] = jnp.transpose(other_d[...])
        for k, part in enumerate((own_ref, psi_1, psi_2, psi_3)):
            owner = lax.rem(me - k + 4, 4)
            for i in range(slots):
                size = sizes[0, slot_sector[owner * slots + i]]
                block = part[i * cap : (i + 1) * cap, :].astype(F32)
                psi_ref[k * slots + i] = jnp.where(support_of(size, cap), block, 0.0).astype(BF16)
        for i in range(slots):
            env = env_ref[i].astype(F32)
            further = other_t[:, i : i + 1] * env * other_d[i : i + 1, :] + other_h[i]
            env_low[i] = jnp.where(core == 0, env, further).astype(BF16)

    result = products(j, me, slot_sector, pair_table, slot_of, left_ref, right_ref, psi_ref, inner)
    result = result + jnp.dot(env_low[j], psi_ref[j], preferred_element_type=F32)
    size = sizes[0, slot_sector[me * slots + j]]
    applied[j] = jnp.where(support_of(size, cap), result, 0.0)

    @pl.when(j == slots - 1)
    def _():
        close_step(slots, psi_ref, precond_ref, applied, a_ref, message_ref)


def later_kernel(
    entries,
    place_ref,
    slot_sector,
    pair_table,
    sizes,
    a_own,
    tile_0,
    msg_1,
    msg_2,
    msg_3,
    half_1,
    half_2,
    half_3,
    before,
    env_low,
    precond_ref,
    left_ref,
    right_ref,
    psi_ref,
    a_ref,
    message_ref,
    applied,
    inner,
    slot_of,
):
    j = pl.program_id(0)
    slots, cap = applied.shape[0], applied.shape[1]
    me = place_ref[0]

    @pl.when(j == 0)
    def _():
        invert_slots(slot_sector, slot_of)
        rows = msg_1.shape[0]
        tiles = [tile_0[...]] + [m[rows - 16 : rows, :] for m in (msg_1, msg_2, msg_3)]
        _, deltas, scale = resolve(tiles, entries)
        for i in range(slots):
            b = (DAMPING / precond_ref[i]) * before[i].astype(F32)
            psi_ref[i] = (scale * (a_own[i] + deltas[0] * b)).astype(BF16)
        for k, (message, half) in enumerate(((msg_1, half_1), (msg_2, half_2), (msg_3, half_3)), 1):
            for i in range(slots):
                a = message[i * cap : (i + 1) * cap, :].astype(F32)
                b = half[i * cap : (i + 1) * cap, :].astype(F32) * before[k * slots + i].astype(F32)
                psi_ref[k * slots + i] = (scale * (a + deltas[k] * b)).astype(BF16)

    result = products(j, me, slot_sector, pair_table, slot_of, left_ref, right_ref, psi_ref, inner)
    result = result + jnp.dot(env_low[j], psi_ref[j], preferred_element_type=F32)
    size = sizes[0, slot_sector[me * slots + j]]
    applied[j] = jnp.where(support_of(size, cap), result, 0.0)

    @pl.when(j == slots - 1)
    def _():
        close_step(slots, psi_ref, precond_ref, applied, a_ref, message_ref)


def fixed(shape):
    return pl.BlockSpec(shape, lambda j: (0,) * len(shape))


def step_cost(left):
    slots, terms, cap, _ = left.shape
    return cost(4 * slots * terms * cap**3, 6 * slots * terms * cap * cap)


def first_step(place, slot_sector, pair_table, sizes, own, got, env, other_h, other_d, precond, left, right):
    slots, terms, cap, _ = left.shape
    rows = slots * cap
    ops = pl.BlockSpec((1, terms, cap, cap), lambda j: (j, 0, 0, 0))
    top = fixed((rows, cap))
    return pl.pallas_call(
        first_kernel,
        grid=(slots,),
        out_shape=[
            jax.ShapeDtypeStruct((4 * slots, cap, cap), BF16),
            jax.ShapeDtypeStruct((slots, cap, cap), BF16),
            jax.ShapeDtypeStruct((slots, cap, cap), F32),
            jax.ShapeDtypeStruct((rows + 16, cap), BF16),
        ],
        in_specs=[whole(SMEM)] * 4
        + [top] * 4
        + [fixed(env.shape), fixed(other_h.shape), fixed(other_d.shape), fixed(precond.shape)]
        + [ops, ops],
        out_specs=[
            fixed((4 * slots, cap, cap)),
            fixed((slots, cap, cap)),
            fixed((slots, cap, cap)),
            fixed((rows + 16, cap)),
        ],
        scratch_shapes=[
            pltpu.VMEM((slots, cap, cap), F32),
            pltpu.VMEM((cap, terms * cap), BF16),
            pltpu.VMEM((cap, slots), F32),
            pltpu.SMEM((slot_sector.shape[0],), jnp.int32),
        ],
        compiler_params=params(),
        cost_estimate=step_cost(left),
        name="first_step",
    )(place, slot_sector, pair_table, sizes, own, *got, env, other_h, other_d, precond, left, right)


def later_step(
    place, slot_sector, pair_table, sizes, a_own, tile, messages, halves, before, env, precond, left, right, last
):
    slots, terms, cap, _ = left.shape
    rows = slots * cap
    ops = pl.BlockSpec((1, terms, cap, cap), lambda j: (j, 0, 0, 0))
    bottom = pl.BlockSpec((rows, cap), lambda j: (1, 0))
    out_rows = 16 if last else rows + 16
    return pl.pallas_call(
        functools.partial(later_kernel, float(slot_sector.shape[0] * cap * cap)),
        grid=(slots,),
        out_shape=[
            jax.ShapeDtypeStruct((4 * slots, cap, cap), BF16),
            jax.ShapeDtypeStruct((slots, cap, cap), F32),
            jax.ShapeDtypeStruct((out_rows, cap), BF16),
        ],
        in_specs=[whole(SMEM)] * 4
        + [fixed(a_own.shape), pl.BlockSpec((16, cap), lambda j: (rows // 16, 0))]
        + [fixed((rows + 16, cap))] * 3
        + [bottom] * 3
        + [fixed(before.shape), fixed(env.shape), fixed(precond.shape)]
        + [ops, ops],
        out_specs=[
            fixed((4 * slots, cap, cap)),
            fixed((slots, cap, cap)),
            fixed((out_rows, cap)),
        ],
        scratch_shapes=[
            pltpu.VMEM((slots, cap, cap), F32),
            pltpu.VMEM((cap, terms * cap), BF16),
            pltpu.SMEM((slot_sector.shape[0],), jnp.int32),
        ],
        compiler_params=params(),
        cost_estimate=step_cost(left),
        name="last_step" if last else "later_step",
    )(place, slot_sector, pair_table, sizes, a_own, tile, *messages, *halves, before, env, precond, left, right)


def ground_kernel(entries, tile_0, tile_1, tile_2, tile_3, a_ref, psi_ref, precond_ref, ground_ref, energy_ref):
    tiles = [t[...] for t in (tile_0, tile_1, tile_2, tile_3)]
    rayleigh, deltas, scale = resolve(tiles, entries)
    energy_ref[0] = rayleigh[0, 0]
    for j in range(a_ref.shape[0]):
        b = (DAMPING / precond_ref[j]) * psi_ref[j].astype(F32)
        ground_ref[j] = (scale * (a_ref[j] + deltas[0] * b)).astype(BF16)


def ground_state(tiles, a_own, psi, precond, entries):
    slots, cap, _ = a_own.shape
    block = fixed((slots, cap, cap))
    return pl.pallas_call(
        functools.partial(ground_kernel, entries),
        grid=(1,),
        out_shape=[
            jax.ShapeDtypeStruct((slots, cap, cap), BF16),
            jax.ShapeDtypeStruct((1,), F32),
        ],
        in_specs=[fixed((16, cap))] * 4 + [block, block, block],
        out_specs=[block, whole(SMEM)],
        compiler_params=params(),
        cost_estimate=cost(4 * slots * cap * cap, 12 * slots * cap * cap),
        name="ground_state",
    )(*tiles, a_own, psi, precond)


def merge_kernel(place_ref, slot_sector, ranks, ground_ref, next_ref, inv_sv, out_ref):
    slots, cap, _ = ground_ref.shape
    lane = lax.broadcasted_iota(jnp.int32, (1, cap), 1)
    live = place_ref[2] != 0
    for j in range(slots):
        rank = ranks[0, slot_sector[place_ref[0] * slots + j]]
        weight = jnp.where(lane < rank, inv_sv[j : j + 1, :] / cap, 0.0)
        scaled = (ground_ref[j].astype(F32) * weight).astype(BF16)
        merged = jnp.dot(scaled, next_ref[j], preferred_element_type=F32)
        out_ref[j] = jnp.where(live, merged, 0.0).astype(BF16)


def merge(place, slot_sector, ranks, ground, following, inv_sv):
    slots, cap, _ = ground.shape
    return pl.pallas_call(
        merge_kernel,
        out_shape=jax.ShapeDtypeStruct((slots, cap, cap), BF16),
        in_specs=[whole(SMEM)] * 3 + [whole()] * 3,
        out_specs=whole(),
        compiler_params=params(),
        cost_estimate=cost(2 * slots * cap**3, 6 * slots * cap * cap),
        name="merge",
    )(place, slot_sector, ranks, ground, following, inv_sv)


def around(value, shift):
    count = lax.axis_size("blk")
    return lax.ppermute(value, "blk", [(i, (i + shift) % count) for i in range(count)])


def three(value):
    return [around(value, shift) for shift in (1, 2, 3)]


def shards(
    psi_guess,
    sector_sizes,
    slot_sector,
    pair_table,
    left_ops,
    right_ops,
    decay,
    source_h,
    precond,
    inv_sv,
    ranks,
):
    sections = lax.axis_size("sect")
    chips = sections // 2
    slots, cap = psi_guess.shape[1], psi_guess.shape[2]
    rows = slots * cap
    entries = float(slot_sector.shape[0] * cap * cap)
    section = lax.axis_index("sect")
    place = jnp.stack(
        [lax.axis_index("blk"), section % 2, (section < sections - 1).astype(jnp.int32), section // 2]
    )
    chip, core = place[3:4], place[1:2]
    left, right = left_ops[0], right_ops[0]

    swap = [(i, i ^ 1) for i in range(sections)]
    other_h = lax.ppermute(source_h[0], "sect", swap)
    other_d = lax.ppermute(decay[0], "sect", swap)

    own_start = start_message(psi_guess.reshape(rows, cap), precond.reshape(rows, cap))
    got_start = three(own_start)

    maps = chip_maps(core, source_h[0], other_h, decay[0], other_d, chips)
    groups = [[2 * q + c for q in range(chips)] for c in range(2)]
    maps = lax.all_to_all(maps, "sect", 0, 0, tiled=True, axis_index_groups=groups)
    env = scan_maps(chip, maps)
    env = lax.all_to_all(env, "sect", 0, 0, tiled=True, axis_index_groups=groups)
    env = env.reshape(slots, cap, cap)

    psi, env_low, a_own, message = first_step(
        place, slot_sector, pair_table, sector_sizes, own_start, got_start, env, other_h, other_d, precond[0], left, right
    )
    for step in range(1, STEPS):
        got = three(message)
        psi, a_own, message = later_step(
            place,
            slot_sector,
            pair_table,
            sector_sizes,
            a_own,
            message,
            got,
            got_start,
            psi,
            env_low,
            precond[0],
            left,
            right,
            step == STEPS - 1,
        )
    tiles = [message] + three(message)
    ground, energies = ground_state(tiles, a_own, psi, precond[0], entries)
    following = lax.ppermute(ground, "sect", [(i + 1, i) for i in range(sections - 1)])
    merged = merge(place, slot_sector, ranks, ground, following, inv_sv[0])
    return (ground[None], energies, merged[None])


def solution(mesh):
    in_specs = (
        P("sect", "blk", None, None),
        P("sect", None),
        P(),
        P(),
        P("sect", "blk", None, None, None),
        P("sect", "blk", None, None, None),
        P("sect", "blk", None),
        P("sect", "blk", None, None),
        P("sect", "blk", None, None),
        P("sect", "blk", None),
        P("sect", None),
    )
    out_specs = (P("sect", "blk", None, None), P("sect"), P("sect", "blk", None, None))
    return jax.shard_map(shards, mesh=mesh, in_specs=in_specs, out_specs=out_specs, check_vma=False)
```

```python
import functools

import jax
import jax.numpy as jnp
from jax import lax
from jax.experimental import pallas as pl
from jax.experimental.pallas import tpu as pltpu
from jax.sharding import PartitionSpec as P

STEPS = 3
DAMPING = 0.5
F32 = jnp.float32
BF16 = jnp.bfloat16
VMEM = pltpu.VMEM
SMEM = pltpu.SMEM
HBM = pltpu.HBM
LIMIT = 20 * 1024 * 1024
SIZES, RANKS, CORE, SOURCES = 0, 64, 96, 128


def params(**more):
    return pltpu.CompilerParams(vmem_limit_bytes=LIMIT, **more)


def whole(space=VMEM):
    return pl.BlockSpec(memory_space=space)


def in_hbm(value):
    return pltpu.with_memory_space_constraint(value, HBM)


def cost(flops, bytes_accessed):
    return pl.CostEstimate(flops=flops, bytes_accessed=bytes_accessed, transcendentals=0)


def start_kernel(
    slot_hbm,
    pair_hbm,
    sizes_hbm,
    ranks_hbm,
    psi_hbm,
    plan,
    out_ref,
    slot_sector,
    pair_table,
    sizes,
    ranks,
    slot_of,
    psi_ref,
    sem,
):
    terms, sectors = pair_table.shape
    slots, cap, _ = out_ref.shape
    me = lax.axis_index("blk")
    moves = (
        (slot_hbm, slot_sector),
        (pair_hbm, pair_table),
        (sizes_hbm, sizes),
        (ranks_hbm, ranks),
        (psi_hbm, psi_ref),
    )
    fetches = [pltpu.make_async_copy(a, b, sem.at[k]) for k, (a, b) in enumerate(moves)]
    for fetch in fetches:
        fetch.start()
    for fetch in fetches:
        fetch.wait()
    plan[CORE] = lax.axis_index("sect") & 1
    for j in range(slots):
        sector = slot_sector[me * slots + j]
        size = sizes[0, sector]
        plan[SIZES + j] = size
        plan[RANKS + j] = ranks[0, sector]
        block = jnp.where(support_of(size, cap), psi_ref[j].astype(F32), 0.0)
        out_ref[j] = block.astype(BF16)
    for slot in range(sectors):
        slot_of[slot_sector[slot]] = slot

    def tables(j, carry):
        sector = slot_sector[me * slots + j]
        for w in range(terms):
            source = slot_of[pair_table[w, sector]]
            plan[SOURCES + j * terms + w] = ((me * slots - (source & -slots)) & (3 * slots)) | (
                source & (slots - 1)
            )
        return carry

    lax.fori_loop(0, slots, tables, 0)


def start(slot_sector, pair_table, sizes, ranks, psi):
    pairs = pair_table.T
    terms = pairs.shape[0]
    slots = psi.shape[0]
    tables = (slot_sector, pairs, sizes, ranks)
    return pl.pallas_call(
        start_kernel,
        out_shape=[
            jax.ShapeDtypeStruct((SOURCES + slots * terms,), jnp.int32),
            jax.ShapeDtypeStruct(psi.shape, BF16),
        ],
        in_specs=[whole(HBM)] * 5,
        out_specs=[whole(SMEM), whole()],
        scratch_shapes=[pltpu.SMEM(t.shape, jnp.int32) for t in tables]
        + [
            pltpu.SMEM(slot_sector.shape, jnp.int32),
            pltpu.VMEM(psi.shape, BF16),
            pltpu.SemaphoreType.DMA((5,)),
        ],
        compiler_params=params(),
        cost_estimate=cost(4 * psi.size, 4 * psi.size),
        name="start",
    )(*[in_hbm(t) for t in tables], in_hbm(psi))


def half_kernel(precond_hbm, out_ref, half_ref, precond_ref, sem):
    slots = precond_ref.shape[0]
    fetches = [
        pltpu.make_async_copy(precond_hbm.at[j], precond_ref.at[j], sem.at[j]) for j in range(slots)
    ]
    for fetch in fetches:
        fetch.start()
    for j in range(slots):
        fetches[j].wait()
        half = DAMPING / precond_ref[j]
        half_ref[j] = half
        out_ref[j] = half.astype(BF16)


def half_message(precond):
    slots, cap, _ = precond.shape
    return pl.pallas_call(
        half_kernel,
        out_shape=[
            jax.ShapeDtypeStruct((slots, cap, cap), BF16),
            jax.ShapeDtypeStruct((slots, cap, cap), F32),
        ],
        in_specs=[whole(HBM)],
        out_specs=[whole(), whole()],
        scratch_shapes=[pltpu.VMEM(precond.shape, F32), pltpu.SemaphoreType.DMA((slots,))],
        compiler_params=params(),
        cost_estimate=cost(2 * slots * cap * cap, 100 * slots * cap * cap),
        name="half_message",
    )(in_hbm(precond))


def chip_kernel(plan, own_hbm, other_h, own_d_hbm, other_d, out_ref, late_t, own_h, own_d, h_sem, d_sem):
    slots, cap = own_d.shape
    mine = slots // 2
    chips, rows, _ = out_ref.shape
    chunk = rows - 8
    cuts = cap // chunk
    core_here = plan[CORE]
    first = core_here * mine
    fetch_d = pltpu.make_async_copy(own_d_hbm, own_d, d_sem)
    fetch_d.start()
    fetches = [
        pltpu.make_async_copy(own_hbm.at[first + j], own_h.at[j], h_sem.at[j]) for j in range(mine)
    ]
    for fetch in fetches:
        fetch.start()
    fetch_d.wait()
    row = lax.broadcasted_iota(jnp.int32, (8, cap), 0)

    def emit(core):
        early_d, late_d = (own_d, other_d) if core == 0 else (other_d, own_d)
        late_t[...] = jnp.transpose(late_d[...])
        whole_d = early_d[...] * late_d[...]
        high = whole_d.astype(BF16).astype(F32)
        low = whole_d - high
        for j in range(mine):
            k = core * mine + j
            tail = jnp.where(
                row == 0, high[k : k + 1, :], jnp.where(row == 1, low[k : k + 1, :], 0.0)
            )
            fetches[j].wait()
            early_h, late_h = (own_h[j], other_h[k]) if core == 0 else (other_h[k], own_h[j])
            both = late_t[:, k : k + 1] * early_h * late_d[k : k + 1, :] + late_h
            for cut in range(cuts):
                part = jnp.concatenate([both[cut * chunk : (cut + 1) * chunk], tail], axis=0)
                out_ref[j * cuts + cut] = part.astype(BF16)

    @pl.when(core_here == 0)
    def _():
        emit(0)

    @pl.when(core_here != 0)
    def _():
        emit(1)


def chip_maps(plan, own_h, other_h, own_d, other_d, chips):
    slots, cap = own_d.shape
    chunk = slots // 2 * cap // chips
    return pl.pallas_call(
        chip_kernel,
        out_shape=jax.ShapeDtypeStruct((chips, chunk + 8, cap), BF16),
        in_specs=[whole(SMEM), whole(HBM), whole(), whole(HBM), whole()],
        out_specs=whole(),
        scratch_shapes=[
            pltpu.VMEM((cap, slots), F32),
            pltpu.VMEM((slots // 2, cap, cap), F32),
            pltpu.VMEM((slots, cap), F32),
            pltpu.SemaphoreType.DMA((slots // 2,)),
            pltpu.SemaphoreType.DMA,
        ],
        compiler_params=params(),
        cost_estimate=cost(2 * slots * cap * cap, 6 * slots * cap * cap),
        name="chip_maps",
    )(plan, in_hbm(own_h), other_h, in_hbm(own_d), other_d)


def scan_kernel(maps_ref, out_ref, factor, factor_t):
    chips, chunk, cap = out_ref.shape
    cuts = cap // chunk
    for z in range(chips):
        tail = maps_ref[z].astype(F32)[chunk : chunk + 8]
        factor[z : z + 1, :] = tail[0:1, :] + tail[1:2, :]
    factor_t[...] = jnp.transpose(factor[...])
    first = pl.multiple_of(lax.rem(lax.axis_index("sect") // 2, cuts) * chunk, chunk)
    columns = factor_t[pl.ds(first, chunk), :]
    state = jnp.zeros((chunk, cap), F32)
    for z in range(chips):
        out_ref[z] = state.astype(BF16)
        source = maps_ref[z].astype(F32)[0:chunk]
        state = columns[:, z : z + 1] * state * factor[z : z + 1, :] + source


def scan_maps(maps):
    chips, rows, cap = maps.shape
    chunk = rows - 8
    return pl.pallas_call(
        scan_kernel,
        out_shape=jax.ShapeDtypeStruct((chips, chunk, cap), BF16),
        in_specs=[whole()],
        out_specs=whole(),
        scratch_shapes=[pltpu.VMEM((chips, cap), F32), pltpu.VMEM((cap, chips), F32)],
        compiler_params=params(),
        cost_estimate=cost(4 * chips * chunk * cap, 200 * chips * chunk * cap),
        name="scan_maps",
    )(maps)


def pack_sums(values, cap):
    row = lax.broadcasted_iota(jnp.int32, (16, cap), 0)
    tile = jnp.zeros((16, cap), F32)
    for k, value in enumerate(values):
        rest = jnp.broadcast_to(value, (16, cap))
        for piece in range(3):
            part = rest.astype(BF16).astype(F32)
            tile = jnp.where(row == 3 * k + piece, part, tile)
            rest = rest - part
    return tile.astype(BF16)


def unpack_sums(tile):
    tile = tile.astype(F32)
    return [
        tile[3 * k : 3 * k + 1] + tile[3 * k + 1 : 3 * k + 2] + tile[3 * k + 2 : 3 * k + 3]
        for k in range(5)
    ]


def local_quotient(numerator, overlap):
    return jnp.where(overlap > 0.0, numerator / jnp.where(overlap > 0.0, overlap, 1.0), 0.0)


def paired(values):
    return (values[0] + values[2]) + (values[1] + values[3])


def resolve(tiles, entries):
    sums = [unpack_sums(tile) for tile in tiles]
    rayleigh = paired([s[0] for s in sums]) / paired([s[1] for s in sums])
    deltas = [rayleigh - local_quotient(s[0], s[1]) for s in sums]
    squares = paired(
        [s[2] + delta * (2.0 * s[3] + delta * s[4]) for s, delta in zip(sums, deltas)]
    )
    scale = lax.rsqrt(squares / entries + 1e-06)
    return rayleigh, deltas, scale


def total(x):
    return jnp.sum(jnp.sum(x, axis=0, keepdims=True), axis=1, keepdims=True)


AHEAD = 3


def fetch_ops(j, left_hbm, right_hbm, left_ref, right_ref, ops_sem):
    pltpu.make_async_copy(left_hbm.at[j], left_ref.at[j], ops_sem.at[0, j]).start()
    pltpu.make_async_copy(right_hbm.at[j], right_ref.at[j], ops_sem.at[1, j]).start()


def fetch_first_ops(*refs):
    for j in range(AHEAD):
        fetch_ops(j, *refs)


def ops_scratch(left, *more):
    return [
        pltpu.VMEM(left.shape, BF16),
        pltpu.VMEM(left.shape, BF16),
        *more,
        pltpu.SemaphoreType.DMA((2, left.shape[0])),
    ]


def products(
    j, plan, left_hbm, right_hbm, left_ref, right_ref, ops_sem, psi_ref, inner
):
    pltpu.make_async_copy(left_hbm.at[j], left_ref.at[j], ops_sem.at[0, j]).wait()
    pltpu.make_async_copy(right_hbm.at[j], right_ref.at[j], ops_sem.at[1, j]).wait()

    @pl.when(j + AHEAD < left_ref.shape[0])
    def _():
        fetch_ops(j + AHEAD, left_hbm, right_hbm, left_ref, right_ref, ops_sem)

    terms, cap = left_ref.shape[1], left_ref.shape[2]
    for w in range(terms):
        inner[:, w * cap : (w + 1) * cap] = jnp.dot(
            left_ref[j, w], psi_ref[plan[SOURCES + j * terms + w]], preferred_element_type=F32
        ).astype(BF16)
    result = jnp.zeros((cap, cap), F32)
    for w in range(0, terms, 2):
        pair = jnp.concatenate([right_ref[j, w], right_ref[j, w + 1]], axis=1)
        result = result + lax.dot_general(
            inner[:, w * cap : (w + 2) * cap],
            pair,
            (((1,), (1,)), ((), ())),
            preferred_element_type=F32,
        )
    return result


def support_of(size, cap):
    row = lax.broadcasted_iota(jnp.int32, (cap, cap), 0)
    column = lax.broadcasted_iota(jnp.int32, (cap, cap), 1)
    return (row < size) & (column < size)


def close_step(slots, psi_ref, half_ref, applied, a_ref, message_ref):
    cap = applied.shape[1]
    zero = jnp.zeros((cap, cap), F32)
    numerator, overlap = zero, zero
    for j in range(slots):
        current = psi_ref[j].astype(F32)
        numerator = numerator + current * applied[j]
        overlap = overlap + current * current
    numerator, overlap = total(numerator), total(overlap)
    quotient = local_quotient(numerator, overlap)
    aa, ab, bb = zero, zero, zero
    for j in range(slots):
        current = psi_ref[j].astype(F32)
        half = half_ref[j]
        a = current - half * (applied[j] - quotient * current)
        b = half * current
        a_ref[j] = a
        if message_ref.shape[0] > 16:
            message_ref[j * cap : (j + 1) * cap, :] = a.astype(BF16)
        aa = aa + a * a
        ab = ab + a * b
        bb = bb + b * b
    sums = [numerator, overlap, total(aa), total(ab), total(bb)]
    rows = message_ref.shape[0]
    message_ref[rows - 16 : rows, :] = pack_sums(sums, cap)


def first_kernel(
    plan,
    psi_0,
    psi_1,
    psi_2,
    psi_3,
    left_hbm,
    right_hbm,
    psi_ref,
    ops_ref,
    inner,
    left_ref,
    right_ref,
    psi_sem,
    ops_sem,
):
    slots, cap = ops_ref.shape[0], ops_ref.shape[1]
    fetches = []
    for k, part in enumerate((psi_0, psi_1, psi_2, psi_3)):
        target = psi_ref.at[pl.ds(k * slots, slots)]
        fetches.append(pltpu.make_async_copy(part, target, psi_sem.at[k]))
    for fetch in fetches:
        fetch.start()
    for fetch in fetches:
        fetch.wait()
    fetch_first_ops(left_hbm, right_hbm, left_ref, right_ref, ops_sem)

    def one(j, carry):
        ops_ref[j] = products(
            j,
            plan,
            left_hbm,
            right_hbm,
            left_ref,
            right_ref,
            ops_sem,
            psi_ref,
            inner,
        )
        return carry

    lax.fori_loop(0, slots, one, 0)


def close_kernel(
    plan,
    psi_ref,
    ops_ref,
    env_own,
    env_got,
    other_h,
    other_d,
    half_ref,
    env_low,
    a_ref,
    message_ref,
    applied,
    other_t,
):
    slots, cap = ops_ref.shape[0], ops_ref.shape[1]
    core = plan[CORE]
    other_t[...] = jnp.transpose(other_d[...])
    for j in range(slots):
        mine = slots // 2
        own, got = env_own[j % mine], env_got[j % mine]
        env = jnp.where(core == j // mine, own.astype(F32), got.astype(F32))
        further = other_t[:, j : j + 1] * env * other_d[j : j + 1, :] + other_h[j]
        env = jnp.where(core == 0, env, further).astype(BF16)
        env_low[j] = env
        result = ops_ref[j] + jnp.dot(env, psi_ref[j], preferred_element_type=F32)
        applied[j] = jnp.where(support_of(plan[SIZES + j], cap), result, 0.0)
    close_step(slots, psi_ref, half_ref, applied, a_ref, message_ref)


def later_kernel(
    entries,
    plan,
    a_own,
    msg_0,
    msg_1,
    msg_2,
    msg_3,
    half_1,
    half_2,
    half_3,
    before,
    env_low,
    half_ref,
    left_hbm,
    right_hbm,
    psi_ref,
    a_ref,
    message_ref,
    applied,
    inner,
    left_ref,
    right_ref,
    ops_sem,
):
    slots, cap = applied.shape[0], applied.shape[1]
    fetch_first_ops(left_hbm, right_hbm, left_ref, right_ref, ops_sem)
    rows = msg_1.shape[0]
    tiles = [m[rows - 16 : rows, :] for m in (msg_0, msg_1, msg_2, msg_3)]
    _, deltas, scale = resolve(tiles, entries)
    for i in range(slots):
        b = half_ref[i] * before[i].astype(F32)
        psi_ref[i] = (scale * (a_own[i] + deltas[0] * b)).astype(BF16)
    for k, (message, half) in enumerate(((msg_1, half_1), (msg_2, half_2), (msg_3, half_3)), 1):
        for i in range(slots):
            a = message[i * cap : (i + 1) * cap, :].astype(F32)
            b = half[i].astype(F32) * before[k * slots + i].astype(F32)
            psi_ref[k * slots + i] = (scale * (a + deltas[k] * b)).astype(BF16)

    def one(j, carry):
        result = products(
            j,
            plan,
            left_hbm,
            right_hbm,
            left_ref,
            right_ref,
            ops_sem,
            psi_ref,
            inner,
        )
        result = result + jnp.dot(env_low[j], psi_ref[j], preferred_element_type=F32)
        applied[j] = jnp.where(support_of(plan[SIZES + j], cap), result, 0.0)
        return carry

    lax.fori_loop(0, slots, one, 0)
    close_step(slots, psi_ref, half_ref, applied, a_ref, message_ref)


def step_cost(left):
    slots, terms, cap, _ = left.shape
    return cost(4 * slots * terms * cap**3, 12 * slots * terms * cap * cap)


def first_products(plan, psi, left, right):
    slots, terms, cap, _ = left.shape
    return pl.pallas_call(
        first_kernel,
        out_shape=[
            jax.ShapeDtypeStruct((4 * slots, cap, cap), BF16),
            jax.ShapeDtypeStruct((slots, cap, cap), F32),
        ],
        in_specs=[whole(SMEM)] + [whole(HBM)] * 6,
        out_specs=[whole()] * 2,
        scratch_shapes=[
            pltpu.VMEM((cap, terms * cap), BF16),
            *ops_scratch(left, pltpu.SemaphoreType.DMA((4,))),
        ],
        compiler_params=params(),
        cost_estimate=cost(cap**3, slots * cap * cap),
        name="first_products",
    )(plan, *[in_hbm(p) for p in psi], in_hbm(left), in_hbm(right))


def first_close(plan, psi, ops, env_own, env_got, other_h, other_d, half):
    slots, cap, _ = ops.shape
    return pl.pallas_call(
        close_kernel,
        out_shape=[
            jax.ShapeDtypeStruct((slots, cap, cap), BF16),
            jax.ShapeDtypeStruct((slots, cap, cap), F32),
            jax.ShapeDtypeStruct((slots * cap + 16, cap), BF16),
        ],
        in_specs=[whole(SMEM)] + [whole()] * 7,
        out_specs=[whole()] * 3,
        scratch_shapes=[
            pltpu.VMEM((slots, cap, cap), F32),
            pltpu.VMEM((cap, slots), F32),
        ],
        compiler_params=params(),
        cost_estimate=cost(2 * slots * cap**3, 20 * slots * cap * cap),
        name="first_close",
    )(plan, psi, ops, env_own, env_got, other_h, other_d, half)


def later_step(
    plan, entries, a_own, message, got, halves, before, env, half, left, right, last
):
    slots, terms, cap, _ = left.shape
    out_rows = 16 if last else slots * cap + 16
    return pl.pallas_call(
        functools.partial(later_kernel, entries),
        out_shape=[
            jax.ShapeDtypeStruct((4 * slots, cap, cap), BF16),
            jax.ShapeDtypeStruct((slots, cap, cap), F32),
            jax.ShapeDtypeStruct((out_rows, cap), BF16),
        ],
        in_specs=[whole(SMEM)] + [whole()] * 11 + [whole(HBM)] * 2,
        out_specs=[whole()] * 3,
        scratch_shapes=[
            pltpu.VMEM((slots, cap, cap), F32),
            pltpu.VMEM((cap, terms * cap), BF16),
            *ops_scratch(left),
        ],
        compiler_params=params(),
        cost_estimate=step_cost(left),
        name="last_step" if last else "later_step",
    )(plan, a_own, message, *got, *halves, before, env, half, in_hbm(left), in_hbm(right))


def ground_kernel(
    entries,
    plan,
    tile_0,
    tile_1,
    tile_2,
    tile_3,
    a_ref,
    psi_ref,
    half_ref,
    inv_sv,
    ground_ref,
    scaled_ref,
    energy_ref,
):
    slots, cap = a_ref.shape[0], a_ref.shape[1]
    lane = lax.broadcasted_iota(jnp.int32, (1, cap), 1)
    tiles = [t[...] for t in (tile_0, tile_1, tile_2, tile_3)]
    rayleigh, deltas, scale = resolve(tiles, entries)
    energy_ref[0] = rayleigh[0, 0]
    for j in range(slots):
        b = half_ref[j] * psi_ref[j].astype(F32)
        ground = (scale * (a_ref[j] + deltas[0] * b)).astype(BF16)
        ground_ref[j] = ground
        weight = jnp.where(lane < plan[RANKS + j], inv_sv[j : j + 1, :] / cap, 0.0)
        scaled_ref[j] = (ground.astype(F32) * weight).astype(BF16)


def ground_state(plan, tiles, a_own, psi, half, inv_sv, entries):
    slots, cap, _ = a_own.shape
    return pl.pallas_call(
        functools.partial(ground_kernel, entries),
        out_shape=[
            jax.ShapeDtypeStruct((slots, cap, cap), BF16),
            jax.ShapeDtypeStruct((slots, cap, cap), BF16),
            jax.ShapeDtypeStruct((1,), F32),
        ],
        in_specs=[whole(SMEM)] + [whole()] * 8,
        out_specs=[whole(), whole(), whole(SMEM)],
        compiler_params=params(),
        cost_estimate=cost(4 * slots * cap * cap, 12 * slots * cap * cap),
        name="ground_state",
    )(plan, *tiles, a_own, psi, half, inv_sv)


def merge_kernel(scaled_ref, next_ref, out_ref):
    live = lax.axis_index("sect") < lax.axis_size("sect") - 1
    for j in range(scaled_ref.shape[0]):
        merged = jnp.dot(scaled_ref[j], next_ref[j], preferred_element_type=F32)
        out_ref[j] = jnp.where(live, merged, 0.0).astype(BF16)


def merge(scaled, following):
    slots, cap, _ = scaled.shape
    return pl.pallas_call(
        merge_kernel,
        out_shape=jax.ShapeDtypeStruct((slots, cap, cap), BF16),
        in_specs=[whole()] * 2,
        out_specs=whole(),
        compiler_params=params(),
        cost_estimate=cost(2 * slots * cap**3, 6 * slots * cap * cap),
        name="merge",
    )(scaled, following)


def around(value, shift):
    count = lax.axis_size("blk")
    return lax.ppermute(value, "blk", [(i, (i + shift) % count) for i in range(count)])


def three(value):
    return [around(value, shift) for shift in (1, 2, 3)]


def shards(
    psi_guess,
    sector_sizes,
    slot_sector,
    pair_table,
    left_ops,
    right_ops,
    decay,
    source_h,
    precond,
    inv_sv,
    ranks,
):
    sections = lax.axis_size("sect")
    chips = sections // 2
    slots, cap = psi_guess.shape[1], psi_guess.shape[2]
    entries = float(slot_sector.shape[0] * cap * cap)
    left, right = left_ops[0], right_ops[0]

    swap = [(i, i ^ 1) for i in range(sections)]
    other_h = lax.ppermute(source_h[0], "sect", swap)
    other_d = lax.ppermute(decay[0], "sect", swap)
    plan, own_psi = start(slot_sector, pair_table, sector_sizes, ranks, psi_guess[0])
    maps = chip_maps(plan, source_h[0], other_h, decay[0], other_d, chips)
    groups = [[2 * q + c for q in range(chips)] for c in range(2)]
    got_maps = lax.all_to_all(maps, "sect", 0, 0, tiled=True, axis_index_groups=groups)
    own_psi, late_precond, _ = lax.optimization_barrier((own_psi, precond[0], maps))
    got_psi = three(own_psi)
    own_half, half = half_message(late_precond)
    halves = three(own_half)
    got_maps, own_half = lax.optimization_barrier((got_maps, own_half))
    env = scan_maps(got_maps)
    got_env = lax.all_to_all(env, "sect", 0, 0, tiled=True, axis_index_groups=groups)
    env_own = got_env.reshape(slots // 2, cap, cap)
    psi, ops = first_products(plan, [own_psi] + got_psi, left, right)
    env_own, ops, halves[1:] = lax.optimization_barrier((env_own, ops, halves[1:]))
    env_got = lax.ppermute(env_own, "sect", swap)
    env_low, a_own, message = first_close(
        plan, psi, ops, env_own, env_got, other_h, other_d, half
    )
    message, halves[0] = lax.optimization_barrier((message, halves[0]))
    for step in range(1, STEPS):
        psi, a_own, message = later_step(
            plan,
            entries,
            a_own,
            message,
            three(message),
            halves,
            psi,
            env_low,
            half,
            left,
            right,
            step == STEPS - 1,
        )
    tiles = [message] + three(message)
    ground, scaled, energies = ground_state(
        plan, tiles, a_own, psi, half, inv_sv[0], entries
    )
    following = lax.ppermute(ground, "sect", [(i + 1, i) for i in range(sections - 1)])
    merged = merge(scaled, following)
    return (ground[None], energies, merged[None])


def solution(mesh):
    in_specs = (
        P("sect", "blk", None, None),
        P("sect", None),
        P(),
        P(),
        P("sect", "blk", None, None, None),
        P("sect", "blk", None, None, None),
        P("sect", "blk", None),
        P("sect", "blk", None, None),
        P("sect", "blk", None, None),
        P("sect", "blk", None),
        P("sect", None),
    )
    out_specs = (P("sect", "blk", None, None), P("sect"), P("sect", "blk", None, None))
    return jax.shard_map(shards, mesh=mesh, in_specs=in_specs, out_specs=out_specs, check_vma=False)
```

```python
import functools

import jax
import jax.numpy as jnp
from jax import lax
from jax.experimental import pallas as pl
from jax.experimental.pallas import tpu as pltpu
from jax.sharding import PartitionSpec as P

STEPS = 3
DAMPING = 0.5
F32 = jnp.float32
BF16 = jnp.bfloat16
VMEM = pltpu.VMEM
SMEM = pltpu.SMEM
HBM = pltpu.HBM
LIMIT = 20 * 1024 * 1024
SIZES, RANKS, CORE, SOURCES = 0, 64, 96, 128


def params(**more):
    return pltpu.CompilerParams(vmem_limit_bytes=LIMIT, **more)


def whole(space=VMEM):
    return pl.BlockSpec(memory_space=space)


def in_hbm(value):
    return pltpu.with_memory_space_constraint(value, HBM)


def cost(flops, bytes_accessed):
    return pl.CostEstimate(flops=flops, bytes_accessed=bytes_accessed, transcendentals=0)


def start_kernel(
    slot_hbm,
    pair_hbm,
    sizes_hbm,
    ranks_hbm,
    psi_hbm,
    h_hbm,
    d_hbm,
    plan,
    out_ref,
    h_ref,
    d_ref,
    slot_sector,
    pair_table,
    sizes,
    ranks,
    slot_of,
    psi_ref,
    sem,
):
    terms, sectors = pair_table.shape
    slots, cap, _ = out_ref.shape
    me = lax.axis_index("blk")
    core = lax.axis_index("sect") & 1
    moves = (
        (slot_hbm, slot_sector),
        (pair_hbm, pair_table),
        (sizes_hbm, sizes),
        (ranks_hbm, ranks),
        (psi_hbm, psi_ref),
        (d_hbm, d_ref),
        (h_hbm.at[pl.ds(core * (slots // 2), slots // 2)], h_ref),
    )
    fetches = [pltpu.make_async_copy(a, b, sem.at[k]) for k, (a, b) in enumerate(moves)]
    for fetch in fetches:
        fetch.start()
    for fetch in fetches[:5]:
        fetch.wait()
    plan[CORE] = core
    for j in range(slots):
        sector = slot_sector[me * slots + j]
        size = sizes[0, sector]
        plan[SIZES + j] = size
        plan[RANKS + j] = ranks[0, sector]
        block = jnp.where(support_of(size, cap), psi_ref[j].astype(F32), 0.0)
        out_ref[j] = block.astype(BF16)
    for slot in range(sectors):
        slot_of[slot_sector[slot]] = slot

    def tables(j, carry):
        sector = slot_sector[me * slots + j]
        for w in range(terms):
            source = slot_of[pair_table[w, sector]]
            plan[SOURCES + j * terms + w] = ((me * slots - (source & -slots)) & (3 * slots)) | (
                source & (slots - 1)
            )
        return carry

    lax.fori_loop(0, slots, tables, 0)
    for fetch in fetches[5:]:
        fetch.wait()


def start(slot_sector, pair_table, sizes, ranks, psi, own_h, own_d):
    pairs = pair_table.T
    terms = pairs.shape[0]
    slots = psi.shape[0]
    tables = (slot_sector, pairs, sizes, ranks)
    return pl.pallas_call(
        start_kernel,
        out_shape=[
            jax.ShapeDtypeStruct((SOURCES + slots * terms,), jnp.int32),
            jax.ShapeDtypeStruct(psi.shape, BF16),
            jax.ShapeDtypeStruct((slots // 2, *psi.shape[1:]), F32),
            jax.ShapeDtypeStruct(own_d.shape, F32),
        ],
        in_specs=[whole(HBM)] * 7,
        out_specs=[whole(SMEM), whole(), whole(), whole()],
        scratch_shapes=[pltpu.SMEM(t.shape, jnp.int32) for t in tables]
        + [
            pltpu.SMEM(slot_sector.shape, jnp.int32),
            pltpu.VMEM(psi.shape, BF16),
            pltpu.SemaphoreType.DMA((7,)),
        ],
        compiler_params=params(),
        cost_estimate=cost(4 * psi.size, 4 * psi.size),
        name="start",
    )(*[in_hbm(t) for t in (*tables, psi, own_h, own_d)])


def half_kernel(precond_hbm, out_ref, half_ref, precond_ref, sem):
    slots = precond_ref.shape[0]
    fetches = [
        pltpu.make_async_copy(precond_hbm.at[j], precond_ref.at[j], sem.at[j]) for j in range(slots)
    ]
    for fetch in fetches:
        fetch.start()
    for j in range(slots):
        fetches[j].wait()
        half = DAMPING / precond_ref[j]
        half_ref[j] = half
        out_ref[j] = half.astype(BF16)


def half_message(precond):
    slots, cap, _ = precond.shape
    return pl.pallas_call(
        half_kernel,
        out_shape=[
            jax.ShapeDtypeStruct((slots, cap, cap), BF16),
            jax.ShapeDtypeStruct((slots, cap, cap), F32),
        ],
        in_specs=[whole(HBM)],
        out_specs=[whole(), whole()],
        scratch_shapes=[pltpu.VMEM(precond.shape, F32), pltpu.SemaphoreType.DMA((slots,))],
        compiler_params=params(),
        cost_estimate=cost(2 * slots * cap * cap, 100 * slots * cap * cap),
        name="half_message",
    )(in_hbm(precond))


def chip_kernel(own_h, other_h, own_d, other_d, out_ref, late_t):
    slots, cap = own_d.shape
    mine = slots // 2
    chips, rows, _ = out_ref.shape
    chunk = rows - 8
    cuts = cap // chunk
    core_here = lax.axis_index("sect") & 1
    row = lax.broadcasted_iota(jnp.int32, (8, cap), 0)

    def emit(core):
        early_d, late_d = (own_d, other_d) if core == 0 else (other_d, own_d)
        late_t[...] = jnp.transpose(late_d[...])
        whole_d = early_d[...] * late_d[...]
        high = whole_d.astype(BF16).astype(F32)
        low = whole_d - high
        for j in range(mine):
            k = core * mine + j
            tail = jnp.where(
                row == 0, high[k : k + 1, :], jnp.where(row == 1, low[k : k + 1, :], 0.0)
            )
            early_h, late_h = (own_h[j], other_h[k]) if core == 0 else (other_h[k], own_h[j])
            both = late_t[:, k : k + 1] * early_h * late_d[k : k + 1, :] + late_h
            for cut in range(cuts):
                part = jnp.concatenate([both[cut * chunk : (cut + 1) * chunk], tail], axis=0)
                out_ref[j * cuts + cut] = part.astype(BF16)

    @pl.when(core_here == 0)
    def _():
        emit(0)

    @pl.when(core_here != 0)
    def _():
        emit(1)


def chip_maps(own_h, other_h, own_d, other_d, chips):
    slots, cap = own_d.shape
    chunk = slots // 2 * cap // chips
    return pl.pallas_call(
        chip_kernel,
        out_shape=jax.ShapeDtypeStruct((chips, chunk + 8, cap), BF16),
        in_specs=[whole()] * 4,
        out_specs=whole(),
        scratch_shapes=[pltpu.VMEM((cap, slots), F32)],
        compiler_params=params(),
        cost_estimate=cost(2 * slots * cap * cap, 6 * slots * cap * cap),
        name="chip_maps",
    )(own_h, other_h, own_d, other_d)


def scan_kernel(maps_ref, out_ref, factor, factor_t):
    chips, chunk, cap = out_ref.shape
    cuts = cap // chunk
    for z in range(chips):
        tail = maps_ref[z].astype(F32)[chunk : chunk + 8]
        factor[z : z + 1, :] = tail[0:1, :] + tail[1:2, :]
    factor_t[...] = jnp.transpose(factor[...])
    first = pl.multiple_of(lax.rem(lax.axis_index("sect") // 2, cuts) * chunk, chunk)
    columns = factor_t[pl.ds(first, chunk), :]
    state = jnp.zeros((chunk, cap), F32)
    for z in range(chips):
        out_ref[z] = state.astype(BF16)
        source = maps_ref[z].astype(F32)[0:chunk]
        state = columns[:, z : z + 1] * state * factor[z : z + 1, :] + source


def scan_maps(maps):
    chips, rows, cap = maps.shape
    chunk = rows - 8
    return pl.pallas_call(
        scan_kernel,
        out_shape=jax.ShapeDtypeStruct((chips, chunk, cap), BF16),
        in_specs=[whole()],
        out_specs=whole(),
        scratch_shapes=[pltpu.VMEM((chips, cap), F32), pltpu.VMEM((cap, chips), F32)],
        compiler_params=params(),
        cost_estimate=cost(4 * chips * chunk * cap, 200 * chips * chunk * cap),
        name="scan_maps",
    )(maps)


def pack_rows(values, cap):
    row = lax.broadcasted_iota(jnp.int32, (16, cap), 0)
    tile = jnp.zeros((16, cap), F32)
    for k, value in enumerate(values):
        rest = jnp.broadcast_to(value, (16, cap))
        for piece in range(3):
            part = rest.astype(BF16).astype(F32)
            tile = jnp.where(row == 3 * k + piece, part, tile)
            rest = rest - part
    return tile.astype(BF16)


def unpack_rows(tile, count):
    tile = tile.astype(F32)
    return [
        tile[3 * k : 3 * k + 1] + tile[3 * k + 1 : 3 * k + 2] + tile[3 * k + 2 : 3 * k + 3]
        for k in range(count)
    ]


def local_quotient(numerator, overlap):
    return jnp.where(overlap > 0.0, numerator / jnp.where(overlap > 0.0, overlap, 1.0), 0.0)


def paired(values):
    return (values[0] + values[2]) + (values[1] + values[3])


def resolve(tiles, entries):
    sums = [unpack_rows(tile, 5) for tile in tiles]
    rayleigh = paired([s[0] for s in sums]) / paired([s[1] for s in sums])
    deltas = [rayleigh - local_quotient(s[0], s[1]) for s in sums]
    squares = paired(
        [s[2] + delta * (2.0 * s[3] + delta * s[4]) for s, delta in zip(sums, deltas)]
    )
    scale = lax.rsqrt(squares / entries + 1e-06)
    return rayleigh, deltas, scale


def total(x):
    return jnp.sum(jnp.sum(x, axis=0, keepdims=True), axis=1, keepdims=True)


AHEAD = 3


def products(j, plan, left_ref, right_ref, psi_ref, inner):
    terms, cap = left_ref.shape[1], left_ref.shape[2]
    for w in range(terms):
        inner[:, w * cap : (w + 1) * cap] = jnp.dot(
            left_ref[j, w], psi_ref[plan[SOURCES + j * terms + w]], preferred_element_type=F32
        ).astype(BF16)
    result = jnp.zeros((cap, cap), F32)
    for w in range(0, terms, 2):
        pair = jnp.concatenate([right_ref[j, w], right_ref[j, w + 1]], axis=1)
        result = result + lax.dot_general(
            inner[:, w * cap : (w + 2) * cap],
            pair,
            (((1,), (1,)), ((), ())),
            preferred_element_type=F32,
        )
    return result


def support_of(size, cap):
    row = lax.broadcasted_iota(jnp.int32, (cap, cap), 0)
    column = lax.broadcasted_iota(jnp.int32, (cap, cap), 1)
    return (row < size) & (column < size)


def close_step(psi_ref, half_ref, applied, a_ref, upper_ref, lower_ref):
    slots, cap, _ = applied.shape
    zero = jnp.zeros((cap, cap), F32)
    numerator, overlap = zero, zero
    for j in range(slots):
        current = psi_ref[j].astype(F32)
        numerator = numerator + current * applied[j]
        overlap = overlap + current * current
    numerator, overlap = total(numerator), total(overlap)
    quotient = local_quotient(numerator, overlap)
    aa, ab, bb = zero, zero, zero
    for j in range(slots):
        current = psi_ref[j].astype(F32)
        half = half_ref[j]
        a = current - half * (applied[j] - quotient * current)
        b = half * current
        a_ref[j] = a
        if upper_ref is None:
            pass
        elif j < slots // 2:
            upper_ref[j * cap : (j + 1) * cap, :] = a.astype(BF16)
        else:
            i = j - slots // 2
            lower_ref[i * cap : (i + 1) * cap, :] = a.astype(BF16)
        aa = aa + a * a
        ab = ab + a * b
        bb = bb + b * b
    sums = [numerator, overlap, total(aa), total(ab), total(bb)]
    rows = lower_ref.shape[0]
    lower_ref[rows - 16 : rows, :] = pack_rows(sums, cap)


def first_kernel(
    plan,
    psi_0,
    psi_1,
    psi_2,
    psi_3,
    left_hbm,
    right_hbm,
    psi_ref,
    ops_ref,
    inner,
    left_ref,
    right_ref,
    psi_sem,
    ops_sem,
):
    slots = psi_0.shape[0]
    fetches = []
    for k, part in enumerate((psi_0, psi_1, psi_2, psi_3)):
        target = psi_ref.at[pl.ds(k * slots, slots)]
        fetches.append(pltpu.make_async_copy(part, target, psi_sem.at[k]))

    def fetch_ops(j):
        return (
            pltpu.make_async_copy(left_hbm.at[j], left_ref.at[j], ops_sem.at[0, j]),
            pltpu.make_async_copy(right_hbm.at[j], right_ref.at[j], ops_sem.at[1, j]),
        )

    def begin(j):
        for copy in fetch_ops(j):
            copy.start()

    for fetch in fetches:
        fetch.start()
    begin(0)
    for fetch in fetches:
        fetch.wait()
    for j in range(1, AHEAD):
        begin(j)

    def one(j, carry):
        for copy in fetch_ops(j):
            copy.wait()

        @pl.when(j + AHEAD < slots)
        def _():
            begin(j + AHEAD)

        ops_ref[j] = products(j, plan, left_ref, right_ref, psi_ref, inner)
        return carry

    lax.fori_loop(0, slots, one, 0)


def close_kernel(
    plan,
    psi_ref,
    ops_ref,
    env_own,
    env_got,
    other_h,
    other_d,
    half_ref,
    env_low,
    a_ref,
    upper_ref,
    lower_ref,
    applied,
    other_t,
):
    slots, cap = applied.shape[0], applied.shape[1]
    core = plan[CORE]
    other_t[...] = jnp.transpose(other_d[...])
    for j in range(slots):
        mine = slots // 2
        own, got = env_own[j % mine], env_got[j % mine]
        env = jnp.where(core == j // mine, own.astype(F32), got.astype(F32))
        further = other_t[:, j : j + 1] * env * other_d[j : j + 1, :] + other_h[j]
        env = jnp.where(core == 0, env, further).astype(BF16)
        env_low[j] = env
        result = ops_ref[j] + jnp.dot(env, psi_ref[j], preferred_element_type=F32)
        applied[j] = jnp.where(support_of(plan[SIZES + j], cap), result, 0.0)
    close_step(psi_ref, half_ref, applied, a_ref, upper_ref, lower_ref)


def later_kernel(
    last,
    entries,
    plan,
    a_own,
    lower_0,
    upper_1,
    lower_1,
    upper_2,
    lower_2,
    upper_3,
    lower_3,
    far_b,
    before,
    env_low,
    half_ref,
    left_ref,
    right_ref,
    psi_ref,
    a_ref,
    *more,
):
    upper_ref = None if last else more[0]
    lower_ref, applied, inner = more[-3:]
    slots, cap = applied.shape[0], applied.shape[1]
    rows = lower_1.shape[0]
    tiles = [m[rows - 16 : rows, :] for m in (lower_0, lower_1, lower_2, lower_3)]
    _, deltas, scale = resolve(tiles, entries)
    for i in range(slots):
        b = half_ref[i] * before[i].astype(F32)
        psi_ref[i] = (scale * (a_own[i] + deltas[0] * b)).astype(BF16)
    received = ((upper_1, lower_1), (upper_2, lower_2), (upper_3, lower_3))
    for k, (upper, lower) in enumerate(received, 1):
        for i in range(slots):
            message, at = (upper, i) if i < slots // 2 else (lower, i - slots // 2)
            a = message[at * cap : (at + 1) * cap, :].astype(F32)
            b = far_b[(k - 1) * slots + i].astype(F32)
            psi_ref[k * slots + i] = (scale * (a + deltas[k] * b)).astype(BF16)

    def one(j, carry):
        result = products(j, plan, left_ref, right_ref, psi_ref, inner)
        result = result + jnp.dot(env_low[j], psi_ref[j], preferred_element_type=F32)
        applied[j] = jnp.where(support_of(plan[SIZES + j], cap), result, 0.0)
        return carry

    lax.fori_loop(0, slots, one, 0)
    close_step(psi_ref, half_ref, applied, a_ref, upper_ref, lower_ref)


def step_cost(left):
    slots, terms, cap, _ = left.shape
    return cost(4 * slots * terms * cap**3, 12 * slots * terms * cap * cap)


def first_products(plan, psi, left, right):
    slots, terms, cap, _ = left.shape
    return pl.pallas_call(
        first_kernel,
        out_shape=[
            jax.ShapeDtypeStruct((4 * slots, cap, cap), BF16),
            jax.ShapeDtypeStruct((slots, cap, cap), F32),
        ],
        in_specs=[whole(SMEM)] + [whole(HBM)] * 6,
        out_specs=[whole()] * 2,
        scratch_shapes=[
            pltpu.VMEM((cap, terms * cap), BF16),
            pltpu.VMEM(left.shape, BF16),
            pltpu.VMEM(right.shape, BF16),
            pltpu.SemaphoreType.DMA((4,)),
            pltpu.SemaphoreType.DMA((2, slots)),
        ],
        compiler_params=params(),
        cost_estimate=cost(cap**3, slots * cap * cap),
        name="first_products",
    )(plan, *[in_hbm(p) for p in psi], in_hbm(left), in_hbm(right))


def ready_kernel(half_1, half_2, half_3, before, left_hbm, b_ref, left_ref, sem):
    slots = half_1.shape[0]
    left_copy = pltpu.make_async_copy(left_hbm, left_ref, sem)
    left_copy.start()
    for k, half in enumerate((half_1, half_2, half_3)):
        for i in range(slots):
            place = (k + 1) * slots + i
            b_ref[k * slots + i] = (half[i].astype(F32) * before[place].astype(F32)).astype(BF16)
    left_copy.wait()


def ready_left(halves, before, left):
    slots, _, cap, _ = left.shape
    return pl.pallas_call(
        ready_kernel,
        out_shape=[
            jax.ShapeDtypeStruct((3 * slots, cap, cap), BF16),
            pltpu.VMEM(left.shape, BF16),
        ],
        in_specs=[whole()] * 4 + [whole(HBM)],
        out_specs=[whole()] * 2,
        scratch_shapes=[pltpu.SemaphoreType.DMA],
        compiler_params=params(),
        cost_estimate=cost(3 * slots * cap * cap, 2 * left.size),
        name="ready_left",
    )(*halves, before, in_hbm(left))


def copy_kernel(right_hbm, right_ref, sem):
    right_copy = pltpu.make_async_copy(right_hbm, right_ref, sem)
    right_copy.start()
    right_copy.wait()


def ready_right(right):
    return pl.pallas_call(
        copy_kernel,
        out_shape=pltpu.VMEM(right.shape, BF16),
        in_specs=[whole(HBM)],
        out_specs=whole(),
        scratch_shapes=[pltpu.SemaphoreType.DMA],
        compiler_params=params(),
        cost_estimate=cost(right.size, 2 * right.size),
        name="ready_right",
    )(in_hbm(right))


def first_close(plan, psi, ops, env_own, env_got, other_h, other_d, half):
    slots, cap, _ = half.shape
    return pl.pallas_call(
        close_kernel,
        out_shape=[
            jax.ShapeDtypeStruct((slots, cap, cap), BF16),
            jax.ShapeDtypeStruct((slots, cap, cap), F32),
            jax.ShapeDtypeStruct((slots // 2 * cap, cap), BF16),
            jax.ShapeDtypeStruct((slots // 2 * cap + 16, cap), BF16),
        ],
        in_specs=[whole(SMEM)] + [whole()] * 7,
        out_specs=[whole()] * 4,
        scratch_shapes=[
            pltpu.VMEM((slots, cap, cap), F32),
            pltpu.VMEM((cap, slots), F32),
        ],
        compiler_params=params(),
        cost_estimate=cost(2 * slots * cap**3, 20 * slots * cap * cap),
        name="first_close",
    )(plan, psi, ops, env_own, env_got, other_h, other_d, half)


def later_step(plan, entries, a_own, lower, got, far_b, before, env, half, left, right, last):
    slots, terms, cap, _ = left.shape
    rows = slots // 2 * cap
    sent = [jax.ShapeDtypeStruct((16 if last else rows + 16, cap), BF16)]
    if not last:
        sent = [jax.ShapeDtypeStruct((rows, cap), BF16)] + sent
    return pl.pallas_call(
        functools.partial(later_kernel, last, entries),
        out_shape=[
            jax.ShapeDtypeStruct((4 * slots, cap, cap), BF16),
            jax.ShapeDtypeStruct((slots, cap, cap), F32),
            *sent,
        ],
        in_specs=[whole(SMEM)] + [whole()] * 14,
        out_specs=[whole()] * (2 + len(sent)),
        scratch_shapes=[
            pltpu.VMEM((slots, cap, cap), F32),
            pltpu.VMEM((cap, terms * cap), BF16),
        ],
        compiler_params=params(),
        cost_estimate=step_cost(left),
        name="last_step" if last else "later_step",
    )(plan, a_own, lower, *got, far_b, before, env, half, left, right)


def near_kernel(a_ref, psi_ref, half_ref, near_ref):
    for j in range(a_ref.shape[0]):
        near_ref[0, j] = a_ref[j].astype(BF16)
        near_ref[1, j] = (half_ref[j] * psi_ref[j].astype(F32)).astype(BF16)


def near_message(a_own, psi, half):
    slots, cap, _ = a_own.shape
    return pl.pallas_call(
        near_kernel,
        out_shape=jax.ShapeDtypeStruct((2, slots, cap, cap), BF16),
        in_specs=[whole()] * 3,
        out_specs=whole(),
        compiler_params=params(),
        cost_estimate=cost(2 * slots * cap * cap, 12 * slots * cap * cap),
        name="near_message",
    )(a_own, psi, half)


def settle_kernel(entries, tile_0, tile_1, tile_2, tile_3, factors_ref, energy_ref):
    tiles = [t[...] for t in (tile_0, tile_1, tile_2, tile_3)]
    rayleigh, deltas, scale = resolve(tiles, entries)
    energy_ref[0] = rayleigh[0, 0]
    factors_ref[...] = pack_rows([scale, deltas[0]], factors_ref.shape[1])


def settle(tiles, entries):
    cap = tiles[0].shape[1]
    return pl.pallas_call(
        functools.partial(settle_kernel, entries),
        out_shape=[jax.ShapeDtypeStruct((16, cap), BF16), jax.ShapeDtypeStruct((1,), F32)],
        in_specs=[whole()] * 4,
        out_specs=[whole(), whole(SMEM)],
        compiler_params=params(),
        cost_estimate=cost(16 * cap, 128 * cap),
        name="settle",
    )(*tiles)


def ground_kernel(plan, factors_ref, a_ref, psi_ref, half_ref, inv_sv, ground_ref, scaled_ref):
    slots, cap = a_ref.shape[0], a_ref.shape[1]
    scale, delta = unpack_rows(factors_ref[...], 2)
    lane = lax.broadcasted_iota(jnp.int32, (1, cap), 1)
    for j in range(slots):
        b = half_ref[j] * psi_ref[j].astype(F32)
        ground = (scale * (a_ref[j] + delta * b)).astype(BF16)
        ground_ref[j] = ground
        weight = jnp.where(lane < plan[RANKS + j], inv_sv[j : j + 1, :] / cap, 0.0)
        scaled_ref[j] = (ground.astype(F32) * weight).astype(BF16)


def ground_state(plan, factors, a_own, psi, half, inv_sv):
    slots, cap, _ = a_own.shape
    return pl.pallas_call(
        ground_kernel,
        out_shape=[jax.ShapeDtypeStruct((slots, cap, cap), BF16)] * 2,
        in_specs=[whole(SMEM)] + [whole()] * 5,
        out_specs=[whole(), whole()],
        compiler_params=params(),
        cost_estimate=cost(4 * slots * cap * cap, 12 * slots * cap * cap),
        name="ground_state",
    )(plan, factors, a_own, psi, half, inv_sv)


def merge_kernel(factors_ref, scaled_ref, near_ref, out_ref):
    live = lax.axis_index("sect") < lax.axis_size("sect") - 1
    scale, delta = unpack_rows(factors_ref[...], 2)
    for j in range(scaled_ref.shape[0]):
        following = scale * (near_ref[0, j].astype(F32) + delta * near_ref[1, j].astype(F32))
        merged = jnp.dot(scaled_ref[j], following.astype(BF16), preferred_element_type=F32)
        out_ref[j] = jnp.where(live, merged, 0.0).astype(BF16)


def merge(factors, scaled, near):
    slots, cap, _ = scaled.shape
    return pl.pallas_call(
        merge_kernel,
        out_shape=jax.ShapeDtypeStruct((slots, cap, cap), BF16),
        in_specs=[whole()] * 3,
        out_specs=whole(),
        compiler_params=params(),
        cost_estimate=cost(2 * slots * cap**3, 6 * slots * cap * cap),
        name="merge",
    )(factors, scaled, near)


def around(value, shift):
    count = lax.axis_size("blk")
    return lax.ppermute(value, "blk", [(i, (i + shift) % count) for i in range(count)])


def three(value):
    return [around(value, shift) for shift in (1, 2, 3)]


def pass_on(upper, lower):
    upper_1 = around(upper, 1)
    lower_3 = around(lower, 3)
    lower_1 = around(lower, 1)
    upper_3 = around(upper, 3)
    upper_2 = around(upper_1, 1)
    lower_2 = around(lower_3, 3)
    return [upper_1, lower_1, upper_2, lower_2, upper_3, lower_3]


def shards(
    psi_guess,
    sector_sizes,
    slot_sector,
    pair_table,
    left_ops,
    right_ops,
    decay,
    source_h,
    precond,
    inv_sv,
    ranks,
):
    sections = lax.axis_size("sect")
    chips = sections // 2
    slots, cap = psi_guess.shape[1], psi_guess.shape[2]
    entries = float(slot_sector.shape[0] * cap * cap)
    left, right = left_ops[0], right_ops[0]

    swap = [(i, i ^ 1) for i in range(sections)]
    other_h = lax.ppermute(source_h[0], "sect", swap)
    other_d = lax.ppermute(decay[0], "sect", swap)
    plan, own_psi, own_h, own_d = start(
        slot_sector, pair_table, sector_sizes, ranks, psi_guess[0], source_h[0], decay[0]
    )
    maps = chip_maps(own_h, other_h, own_d, other_d, chips)
    groups = [[2 * q + c for q in range(chips)] for c in range(2)]
    got_maps = lax.all_to_all(maps, "sect", 0, 0, tiled=True, axis_index_groups=groups)
    own_psi, late_precond, _ = lax.optimization_barrier((own_psi, precond[0], maps))
    got_psi = three(own_psi)
    own_half, half = half_message(late_precond)
    halves = three(own_half)
    got_maps, own_half = lax.optimization_barrier((got_maps, own_half))
    env = scan_maps(got_maps)
    got_env = lax.all_to_all(env, "sect", 0, 0, tiled=True, axis_index_groups=groups)
    env_own = got_env.reshape(slots // 2, cap, cap)
    psi, ops = first_products(plan, [own_psi] + got_psi, left, right)
    env_own, ops, halves[1:] = lax.optimization_barrier((env_own, ops, halves[1:]))
    env_got = lax.ppermute(env_own, "sect", swap)
    env_low, a_own, upper, lower = first_close(
        plan, psi, ops, env_own, env_got, other_h, other_d, half
    )
    lower, halves[0] = lax.optimization_barrier((lower, halves[0]))
    for step in range(1, STEPS):
        last = step == STEPS - 1
        got = pass_on(upper, lower)
        later_left, later_right, _ = lax.optimization_barrier((left, right, lower))
        far_b, later_left = ready_left(halves, psi, later_left)
        later_right = ready_right(later_right)
        psi, a_own, *sent = later_step(
            plan, entries, a_own, lower, got, far_b, psi, env_low, half, later_left, later_right, last
        )
        upper, lower = sent[0], sent[-1]
    tile = lower
    near = near_message(a_own, psi, half)
    behind = [(i + 1, i) for i in range(sections - 1)]
    near = lax.ppermute(near, "sect", behind)
    factors, energies = settle([tile] + three(tile), entries)
    near_factors = lax.ppermute(factors, "sect", behind)
    ground, scaled = ground_state(plan, factors, a_own, psi, half, inv_sv[0])
    merged = merge(near_factors, scaled, near)
    return (ground[None], energies, merged[None])


def solution(mesh):
    in_specs = (
        P("sect", "blk", None, None),
        P("sect", None),
        P(),
        P(),
        P("sect", "blk", None, None, None),
        P("sect", "blk", None, None, None),
        P("sect", "blk", None),
        P("sect", "blk", None, None),
        P("sect", "blk", None, None),
        P("sect", "blk", None),
        P("sect", None),
    )
    out_specs = (P("sect", "blk", None, None), P("sect"), P("sect", "blk", None, None))
    return jax.shard_map(shards, mesh=mesh, in_specs=in_specs, out_specs=out_specs, check_vma=False)
```

```python
import functools

import jax
import jax.numpy as jnp
from jax import lax
from jax.experimental import pallas as pl
from jax.experimental.pallas import tpu as pltpu
from jax.sharding import PartitionSpec as P

STEPS = 3
DAMPING = 0.5
F32 = jnp.float32
BF16 = jnp.bfloat16
VMEM = pltpu.VMEM
SMEM = pltpu.SMEM
HBM = pltpu.HBM
LIMIT = 20 * 1024 * 1024
SIZES, RANKS, CORE, SOURCES = 0, 64, 96, 128


def params(**more):
    return pltpu.CompilerParams(vmem_limit_bytes=LIMIT, **more)


def whole(space=VMEM):
    return pl.BlockSpec(memory_space=space)


def in_hbm(value):
    return pltpu.with_memory_space_constraint(value, HBM)


def cost(flops, bytes_accessed):
    return pl.CostEstimate(flops=flops, bytes_accessed=bytes_accessed, transcendentals=0)


def start_kernel(
    slot_hbm,
    pair_hbm,
    sizes_hbm,
    ranks_hbm,
    psi_hbm,
    h_hbm,
    d_hbm,
    precond_hbm,
    plan,
    out_ref,
    h_ref,
    d_ref,
    precond_ref,
    slot_sector,
    pair_table,
    sizes,
    ranks,
    slot_of,
    psi_ref,
    sem,
):
    terms, sectors = pair_table.shape
    slots, cap, _ = out_ref.shape
    me = lax.axis_index("blk")
    core = lax.axis_index("sect") & 1
    moves = (
        (slot_hbm, slot_sector),
        (pair_hbm, pair_table),
        (sizes_hbm, sizes),
        (ranks_hbm, ranks),
        (psi_hbm, psi_ref),
        (d_hbm, d_ref),
        (h_hbm.at[pl.ds(core * (slots // 2), slots // 2)], h_ref),
        (precond_hbm, precond_ref),
    )
    fetches = [pltpu.make_async_copy(a, b, sem.at[k]) for k, (a, b) in enumerate(moves)]
    for fetch in fetches:
        fetch.start()
    for fetch in fetches[:5]:
        fetch.wait()
    plan[CORE] = core
    for j in range(slots):
        sector = slot_sector[me * slots + j]
        size = sizes[0, sector]
        plan[SIZES + j] = size
        plan[RANKS + j] = ranks[0, sector]
        block = jnp.where(support_of(size, cap), psi_ref[j].astype(F32), 0.0)
        out_ref[j] = block.astype(BF16)
    for slot in range(sectors):
        slot_of[slot_sector[slot]] = slot

    def tables(j, carry):
        sector = slot_sector[me * slots + j]
        for w in range(terms):
            source = slot_of[pair_table[w, sector]]
            plan[SOURCES + j * terms + w] = ((me * slots - (source & -slots)) & (3 * slots)) | (
                source & (slots - 1)
            )
        return carry

    lax.fori_loop(0, slots, tables, 0)
    for fetch in fetches[5:]:
        fetch.wait()


def start(slot_sector, pair_table, sizes, ranks, psi, own_h, own_d, precond):
    pairs = pair_table.T
    terms = pairs.shape[0]
    slots = psi.shape[0]
    tables = (slot_sector, pairs, sizes, ranks)
    return pl.pallas_call(
        start_kernel,
        out_shape=[
            jax.ShapeDtypeStruct((SOURCES + slots * terms,), jnp.int32),
            jax.ShapeDtypeStruct(psi.shape, BF16),
            jax.ShapeDtypeStruct((slots // 2, *psi.shape[1:]), F32),
            jax.ShapeDtypeStruct(own_d.shape, F32),
            pltpu.VMEM(precond.shape, F32),
        ],
        in_specs=[whole(HBM)] * 8,
        out_specs=[whole(SMEM), whole(), whole(), whole(), whole()],
        scratch_shapes=[pltpu.SMEM(t.shape, jnp.int32) for t in tables]
        + [
            pltpu.SMEM(slot_sector.shape, jnp.int32),
            pltpu.VMEM(psi.shape, BF16),
            pltpu.SemaphoreType.DMA((8,)),
        ],
        compiler_params=params(),
        cost_estimate=cost(4 * psi.size, 4 * psi.size),
        name="start",
    )(*[in_hbm(t) for t in (*tables, psi, own_h, own_d, precond)])


def half_kernel(precond_ref, out_ref, half_ref):
    for j in range(precond_ref.shape[0]):
        half = DAMPING / precond_ref[j]
        half_ref[j] = half
        out_ref[j] = half.astype(BF16)


def half_message(precond):
    slots, cap, _ = precond.shape
    return pl.pallas_call(
        half_kernel,
        out_shape=[
            jax.ShapeDtypeStruct((slots, cap, cap), BF16),
            jax.ShapeDtypeStruct((slots, cap, cap), F32),
        ],
        in_specs=[whole()],
        out_specs=[whole(), whole()],
        compiler_params=params(),
        cost_estimate=cost(2 * slots * cap * cap, 100 * slots * cap * cap),
        name="half_message",
    )(precond)


def chip_kernel(own_h, other_h, own_d, other_d, out_ref, late_t):
    slots, cap = own_d.shape
    mine = slots // 2
    chips, rows, _ = out_ref.shape
    chunk = rows - 8
    cuts = cap // chunk
    core_here = lax.axis_index("sect") & 1
    row = lax.broadcasted_iota(jnp.int32, (8, cap), 0)

    def emit(core):
        early_d, late_d = (own_d, other_d) if core == 0 else (other_d, own_d)
        late_t[...] = jnp.transpose(late_d[...])
        whole_d = early_d[...] * late_d[...]
        high = whole_d.astype(BF16).astype(F32)
        low = whole_d - high
        for j in range(mine):
            k = core * mine + j
            tail = jnp.where(
                row == 0, high[k : k + 1, :], jnp.where(row == 1, low[k : k + 1, :], 0.0)
            )
            early_h, late_h = (own_h[j], other_h[k]) if core == 0 else (other_h[k], own_h[j])
            both = late_t[:, k : k + 1] * early_h * late_d[k : k + 1, :] + late_h
            for cut in range(cuts):
                part = jnp.concatenate([both[cut * chunk : (cut + 1) * chunk], tail], axis=0)
                out_ref[j * cuts + cut] = part.astype(BF16)

    @pl.when(core_here == 0)
    def _():
        emit(0)

    @pl.when(core_here != 0)
    def _():
        emit(1)


def chip_maps(own_h, other_h, own_d, other_d, chips):
    slots, cap = own_d.shape
    chunk = slots // 2 * cap // chips
    return pl.pallas_call(
        chip_kernel,
        out_shape=jax.ShapeDtypeStruct((chips, chunk + 8, cap), BF16),
        in_specs=[whole()] * 4,
        out_specs=whole(),
        scratch_shapes=[pltpu.VMEM((cap, slots), F32)],
        compiler_params=params(),
        cost_estimate=cost(2 * slots * cap * cap, 6 * slots * cap * cap),
        name="chip_maps",
    )(own_h, other_h, own_d, other_d)


def scan_kernel(maps_ref, out_ref, factor, factor_t):
    chips, chunk, cap = out_ref.shape
    cuts = cap // chunk
    for z in range(chips):
        tail = maps_ref[z].astype(F32)[chunk : chunk + 8]
        factor[z : z + 1, :] = tail[0:1, :] + tail[1:2, :]
    factor_t[...] = jnp.transpose(factor[...])
    first = pl.multiple_of(lax.rem(lax.axis_index("sect") // 2, cuts) * chunk, chunk)
    columns = factor_t[pl.ds(first, chunk), :]
    state = jnp.zeros((chunk, cap), F32)
    for z in range(chips):
        out_ref[z] = state.astype(BF16)
        source = maps_ref[z].astype(F32)[0:chunk]
        state = columns[:, z : z + 1] * state * factor[z : z + 1, :] + source


def scan_maps(maps):
    chips, rows, cap = maps.shape
    chunk = rows - 8
    return pl.pallas_call(
        scan_kernel,
        out_shape=jax.ShapeDtypeStruct((chips, chunk, cap), BF16),
        in_specs=[whole()],
        out_specs=whole(),
        scratch_shapes=[pltpu.VMEM((chips, cap), F32), pltpu.VMEM((cap, chips), F32)],
        compiler_params=params(),
        cost_estimate=cost(4 * chips * chunk * cap, 200 * chips * chunk * cap),
        name="scan_maps",
    )(maps)


def pack_rows(values, cap):
    row = lax.broadcasted_iota(jnp.int32, (16, cap), 0)
    tile = jnp.zeros((16, cap), F32)
    for k, value in enumerate(values):
        rest = jnp.broadcast_to(value, (16, cap))
        for piece in range(3):
            part = rest.astype(BF16).astype(F32)
            tile = jnp.where(row == 3 * k + piece, part, tile)
            rest = rest - part
    return tile.astype(BF16)


def unpack_rows(tile, count):
    tile = tile.astype(F32)
    return [
        tile[3 * k : 3 * k + 1] + tile[3 * k + 1 : 3 * k + 2] + tile[3 * k + 2 : 3 * k + 3]
        for k in range(count)
    ]


def local_quotient(numerator, overlap):
    return jnp.where(overlap > 0.0, numerator / jnp.where(overlap > 0.0, overlap, 1.0), 0.0)


def paired(values):
    return (values[0] + values[2]) + (values[1] + values[3])


def resolve(tiles, entries):
    sums = [unpack_rows(tile, 5) for tile in tiles]
    rayleigh = paired([s[0] for s in sums]) / paired([s[1] for s in sums])
    deltas = [rayleigh - local_quotient(s[0], s[1]) for s in sums]
    squares = paired(
        [s[2] + delta * (2.0 * s[3] + delta * s[4]) for s, delta in zip(sums, deltas)]
    )
    scale = lax.rsqrt(squares / entries + 1e-06)
    return rayleigh, deltas, scale


def total(x):
    return jnp.sum(jnp.sum(x, axis=0, keepdims=True), axis=1, keepdims=True)


AHEAD = 3


def products(j, plan, left_ref, right_ref, psi_ref, inner):
    terms, cap = left_ref.shape[1], left_ref.shape[2]
    for w in range(terms):
        inner[:, w * cap : (w + 1) * cap] = jnp.dot(
            left_ref[j, w], psi_ref[plan[SOURCES + j * terms + w]], preferred_element_type=F32
        ).astype(BF16)
    result = jnp.zeros((cap, cap), F32)
    for w in range(0, terms, 2):
        pair = jnp.concatenate([right_ref[j, w], right_ref[j, w + 1]], axis=1)
        result = result + lax.dot_general(
            inner[:, w * cap : (w + 2) * cap],
            pair,
            (((1,), (1,)), ((), ())),
            preferred_element_type=F32,
        )
    return result


def support_of(size, cap):
    row = lax.broadcasted_iota(jnp.int32, (cap, cap), 0)
    column = lax.broadcasted_iota(jnp.int32, (cap, cap), 1)
    return (row < size) & (column < size)


def close_step(psi_ref, half_ref, applied, a_ref, upper_ref, lower_ref):
    slots, cap, _ = applied.shape
    zero = jnp.zeros((cap, cap), F32)
    numerator, overlap = zero, zero
    for j in range(slots):
        current = psi_ref[j].astype(F32)
        numerator = numerator + current * applied[j]
        overlap = overlap + current * current
    numerator, overlap = total(numerator), total(overlap)
    quotient = local_quotient(numerator, overlap)
    aa, ab, bb = zero, zero, zero
    for j in range(slots):
        current = psi_ref[j].astype(F32)
        half = half_ref[j]
        a = current - half * (applied[j] - quotient * current)
        b = half * current
        a_ref[j] = a
        if upper_ref is None:
            pass
        elif j < slots // 2:
            upper_ref[j * cap : (j + 1) * cap, :] = a.astype(BF16)
        else:
            i = j - slots // 2
            lower_ref[i * cap : (i + 1) * cap, :] = a.astype(BF16)
        aa = aa + a * a
        ab = ab + a * b
        bb = bb + b * b
    sums = [numerator, overlap, total(aa), total(ab), total(bb)]
    rows = lower_ref.shape[0]
    lower_ref[rows - 16 : rows, :] = pack_rows(sums, cap)


def first_kernel(
    plan,
    psi_0,
    psi_1,
    psi_2,
    psi_3,
    left_hbm,
    right_hbm,
    psi_ref,
    ops_ref,
    inner,
    left_ref,
    right_ref,
    psi_sem,
    ops_sem,
):
    slots = psi_0.shape[0]
    fetches = []
    for k, part in enumerate((psi_0, psi_1, psi_2, psi_3)):
        target = psi_ref.at[pl.ds(k * slots, slots)]
        fetches.append(pltpu.make_async_copy(part, target, psi_sem.at[k]))

    def fetch_ops(j):
        return (
            pltpu.make_async_copy(left_hbm.at[j], left_ref.at[j], ops_sem.at[0, j]),
            pltpu.make_async_copy(right_hbm.at[j], right_ref.at[j], ops_sem.at[1, j]),
        )

    def begin(j):
        for copy in fetch_ops(j):
            copy.start()

    for fetch in fetches:
        fetch.start()
    begin(0)
    for fetch in fetches:
        fetch.wait()
    for j in range(1, AHEAD):
        begin(j)

    def one(j, carry):
        for copy in fetch_ops(j):
            copy.wait()

        @pl.when(j + AHEAD < slots)
        def _():
            begin(j + AHEAD)

        ops_ref[j] = products(j, plan, left_ref, right_ref, psi_ref, inner)
        return carry

    lax.fori_loop(0, slots, one, 0)


def close_kernel(
    plan,
    psi_ref,
    ops_ref,
    env_own,
    env_got,
    other_h,
    other_d,
    half_ref,
    env_low,
    a_ref,
    upper_ref,
    lower_ref,
    applied,
    other_t,
):
    slots, cap = applied.shape[0], applied.shape[1]
    core = plan[CORE]
    other_t[...] = jnp.transpose(other_d[...])
    for j in range(slots):
        mine = slots // 2
        own, got = env_own[j % mine], env_got[j % mine]
        env = jnp.where(core == j // mine, own.astype(F32), got.astype(F32))
        further = other_t[:, j : j + 1] * env * other_d[j : j + 1, :] + other_h[j]
        env = jnp.where(core == 0, env, further).astype(BF16)
        env_low[j] = env
        result = ops_ref[j] + jnp.dot(env, psi_ref[j], preferred_element_type=F32)
        applied[j] = jnp.where(support_of(plan[SIZES + j], cap), result, 0.0)
    close_step(psi_ref, half_ref, applied, a_ref, upper_ref, lower_ref)


def later_kernel(
    last,
    entries,
    plan,
    a_own,
    lower_0,
    upper_1,
    lower_1,
    upper_2,
    lower_2,
    upper_3,
    lower_3,
    far_b,
    before,
    env_low,
    half_ref,
    left_ref,
    right_ref,
    psi_ref,
    a_ref,
    *more,
):
    upper_ref = None if last else more[0]
    lower_ref, applied, inner = more[-3:]
    slots, cap = applied.shape[0], applied.shape[1]
    rows = lower_1.shape[0]
    tiles = [m[rows - 16 : rows, :] for m in (lower_0, lower_1, lower_2, lower_3)]
    _, deltas, scale = resolve(tiles, entries)
    for i in range(slots):
        b = half_ref[i] * before[i].astype(F32)
        psi_ref[i] = (scale * (a_own[i] + deltas[0] * b)).astype(BF16)
    received = ((upper_1, lower_1), (upper_2, lower_2), (upper_3, lower_3))
    for k, (upper, lower) in enumerate(received, 1):
        for i in range(slots):
            message, at = (upper, i) if i < slots // 2 else (lower, i - slots // 2)
            a = message[at * cap : (at + 1) * cap, :].astype(F32)
            b = far_b[(k - 1) * slots + i].astype(F32)
            psi_ref[k * slots + i] = (scale * (a + deltas[k] * b)).astype(BF16)

    def one(j, carry):
        result = products(j, plan, left_ref, right_ref, psi_ref, inner)
        result = result + jnp.dot(env_low[j], psi_ref[j], preferred_element_type=F32)
        applied[j] = jnp.where(support_of(plan[SIZES + j], cap), result, 0.0)
        return carry

    lax.fori_loop(0, slots, one, 0)
    close_step(psi_ref, half_ref, applied, a_ref, upper_ref, lower_ref)


def step_cost(left):
    slots, terms, cap, _ = left.shape
    return cost(4 * slots * terms * cap**3, 12 * slots * terms * cap * cap)


def first_products(plan, psi, left, right):
    slots, terms, cap, _ = left.shape
    return pl.pallas_call(
        first_kernel,
        out_shape=[
            jax.ShapeDtypeStruct((4 * slots, cap, cap), BF16),
            jax.ShapeDtypeStruct((slots, cap, cap), F32),
        ],
        in_specs=[whole(SMEM)] + [whole(HBM)] * 6,
        out_specs=[whole()] * 2,
        scratch_shapes=[
            pltpu.VMEM((cap, terms * cap), BF16),
            pltpu.VMEM(left.shape, BF16),
            pltpu.VMEM(right.shape, BF16),
            pltpu.SemaphoreType.DMA((4,)),
            pltpu.SemaphoreType.DMA((2, slots)),
        ],
        compiler_params=params(),
        cost_estimate=cost(cap**3, slots * cap * cap),
        name="first_products",
    )(plan, *[in_hbm(p) for p in psi], in_hbm(left), in_hbm(right))


def ready_kernel(half_1, half_2, half_3, before, left_hbm, b_ref, left_ref, sem):
    slots = half_1.shape[0]
    left_copy = pltpu.make_async_copy(left_hbm, left_ref, sem)
    left_copy.start()
    for k, half in enumerate((half_1, half_2, half_3)):
        for i in range(slots):
            place = (k + 1) * slots + i
            b_ref[k * slots + i] = (half[i].astype(F32) * before[place].astype(F32)).astype(BF16)
    left_copy.wait()


def ready_left(halves, before, left):
    slots, _, cap, _ = left.shape
    return pl.pallas_call(
        ready_kernel,
        out_shape=[
            jax.ShapeDtypeStruct((3 * slots, cap, cap), BF16),
            pltpu.VMEM(left.shape, BF16),
        ],
        in_specs=[whole()] * 4 + [whole(HBM)],
        out_specs=[whole()] * 2,
        scratch_shapes=[pltpu.SemaphoreType.DMA],
        compiler_params=params(),
        cost_estimate=cost(3 * slots * cap * cap, 2 * left.size),
        name="ready_left",
    )(*halves, before, in_hbm(left))


def copy_kernel(right_hbm, right_ref, sem):
    right_copy = pltpu.make_async_copy(right_hbm, right_ref, sem)
    right_copy.start()
    right_copy.wait()


def ready_right(right):
    return pl.pallas_call(
        copy_kernel,
        out_shape=pltpu.VMEM(right.shape, BF16),
        in_specs=[whole(HBM)],
        out_specs=whole(),
        scratch_shapes=[pltpu.SemaphoreType.DMA],
        compiler_params=params(),
        cost_estimate=cost(right.size, 2 * right.size),
        name="ready_right",
    )(in_hbm(right))


def first_close(plan, psi, ops, env_own, env_got, other_h, other_d, half):
    slots, cap, _ = half.shape
    return pl.pallas_call(
        close_kernel,
        out_shape=[
            jax.ShapeDtypeStruct((slots, cap, cap), BF16),
            jax.ShapeDtypeStruct((slots, cap, cap), F32),
            jax.ShapeDtypeStruct((slots // 2 * cap, cap), BF16),
            jax.ShapeDtypeStruct((slots // 2 * cap + 16, cap), BF16),
        ],
        in_specs=[whole(SMEM)] + [whole()] * 7,
        out_specs=[whole()] * 4,
        scratch_shapes=[
            pltpu.VMEM((slots, cap, cap), F32),
            pltpu.VMEM((cap, slots), F32),
        ],
        compiler_params=params(),
        cost_estimate=cost(2 * slots * cap**3, 20 * slots * cap * cap),
        name="first_close",
    )(plan, psi, ops, env_own, env_got, other_h, other_d, half)


def later_step(plan, entries, a_own, lower, got, far_b, before, env, half, left, right, last):
    slots, terms, cap, _ = left.shape
    rows = slots // 2 * cap
    sent = [jax.ShapeDtypeStruct((16 if last else rows + 16, cap), BF16)]
    if not last:
        sent = [jax.ShapeDtypeStruct((rows, cap), BF16)] + sent
    return pl.pallas_call(
        functools.partial(later_kernel, last, entries),
        out_shape=[
            jax.ShapeDtypeStruct((4 * slots, cap, cap), BF16),
            jax.ShapeDtypeStruct((slots, cap, cap), F32),
            *sent,
        ],
        in_specs=[whole(SMEM)] + [whole()] * 14,
        out_specs=[whole()] * (2 + len(sent)),
        scratch_shapes=[
            pltpu.VMEM((slots, cap, cap), F32),
            pltpu.VMEM((cap, terms * cap), BF16),
        ],
        compiler_params=params(),
        cost_estimate=step_cost(left),
        name="last_step" if last else "later_step",
    )(plan, a_own, lower, *got, far_b, before, env, half, left, right)


def near_kernel(a_ref, psi_ref, half_ref, near_ref):
    for j in range(a_ref.shape[0]):
        near_ref[0, j] = a_ref[j].astype(BF16)
        near_ref[1, j] = (half_ref[j] * psi_ref[j].astype(F32)).astype(BF16)


def near_message(a_own, psi, half):
    slots, cap, _ = a_own.shape
    return pl.pallas_call(
        near_kernel,
        out_shape=jax.ShapeDtypeStruct((2, slots, cap, cap), BF16),
        in_specs=[whole()] * 3,
        out_specs=whole(),
        compiler_params=params(),
        cost_estimate=cost(2 * slots * cap * cap, 12 * slots * cap * cap),
        name="near_message",
    )(a_own, psi, half)


def settle_kernel(entries, tile_0, tile_1, tile_2, tile_3, factors_ref, energy_ref):
    tiles = [t[...] for t in (tile_0, tile_1, tile_2, tile_3)]
    rayleigh, deltas, scale = resolve(tiles, entries)
    energy_ref[0] = rayleigh[0, 0]
    factors_ref[...] = pack_rows([scale, deltas[0]], factors_ref.shape[1])


def settle(tiles, entries):
    cap = tiles[0].shape[1]
    return pl.pallas_call(
        functools.partial(settle_kernel, entries),
        out_shape=[jax.ShapeDtypeStruct((16, cap), BF16), jax.ShapeDtypeStruct((1,), F32)],
        in_specs=[whole()] * 4,
        out_specs=[whole(), whole(SMEM)],
        compiler_params=params(),
        cost_estimate=cost(16 * cap, 128 * cap),
        name="settle",
    )(*tiles)


def ground_kernel(plan, factors_ref, a_ref, psi_ref, half_ref, inv_sv, ground_ref, scaled_ref):
    slots, cap = a_ref.shape[0], a_ref.shape[1]
    scale, delta = unpack_rows(factors_ref[...], 2)
    lane = lax.broadcasted_iota(jnp.int32, (1, cap), 1)
    for j in range(slots):
        b = half_ref[j] * psi_ref[j].astype(F32)
        ground = (scale * (a_ref[j] + delta * b)).astype(BF16)
        ground_ref[j] = ground
        weight = jnp.where(lane < plan[RANKS + j], inv_sv[j : j + 1, :] / cap, 0.0)
        scaled_ref[j] = (ground.astype(F32) * weight).astype(BF16)


def ground_state(plan, factors, a_own, psi, half, inv_sv):
    slots, cap, _ = a_own.shape
    return pl.pallas_call(
        ground_kernel,
        out_shape=[jax.ShapeDtypeStruct((slots, cap, cap), BF16)] * 2,
        in_specs=[whole(SMEM)] + [whole()] * 5,
        out_specs=[whole(), whole()],
        compiler_params=params(),
        cost_estimate=cost(4 * slots * cap * cap, 12 * slots * cap * cap),
        name="ground_state",
    )(plan, factors, a_own, psi, half, inv_sv)


def merge_kernel(factors_ref, scaled_ref, near_ref, out_ref):
    live = lax.axis_index("sect") < lax.axis_size("sect") - 1
    scale, delta = unpack_rows(factors_ref[...], 2)
    for j in range(scaled_ref.shape[0]):
        following = scale * (near_ref[0, j].astype(F32) + delta * near_ref[1, j].astype(F32))
        merged = jnp.dot(scaled_ref[j], following.astype(BF16), preferred_element_type=F32)
        out_ref[j] = jnp.where(live, merged, 0.0).astype(BF16)


def merge(factors, scaled, near):
    slots, cap, _ = scaled.shape
    return pl.pallas_call(
        merge_kernel,
        out_shape=jax.ShapeDtypeStruct((slots, cap, cap), BF16),
        in_specs=[whole()] * 3,
        out_specs=whole(),
        compiler_params=params(),
        cost_estimate=cost(2 * slots * cap**3, 6 * slots * cap * cap),
        name="merge",
    )(factors, scaled, near)


def around(value, shift):
    count = lax.axis_size("blk")
    return lax.ppermute(value, "blk", [(i, (i + shift) % count) for i in range(count)])


def three(value):
    return [around(value, shift) for shift in (1, 2, 3)]


def pass_on(upper, lower, beside):
    upper_1 = around(upper, 1)
    lower_3 = around(lower, 3)
    lower_1 = around(lower, 1)
    upper_3 = around(upper, 3)
    done = list(beside())
    lower_3, done[0] = lax.optimization_barrier((lower_3, done[0]))
    upper_1, upper_3 = lax.optimization_barrier((upper_1, upper_3))
    upper_2 = around(upper_1, 1)
    lower_2 = around(lower_3, 3)
    return [upper_1, lower_1, upper_2, lower_2, upper_3, lower_3], done


def shards(
    psi_guess,
    sector_sizes,
    slot_sector,
    pair_table,
    left_ops,
    right_ops,
    decay,
    source_h,
    precond,
    inv_sv,
    ranks,
):
    sections = lax.axis_size("sect")
    chips = sections // 2
    slots, cap = psi_guess.shape[1], psi_guess.shape[2]
    entries = float(slot_sector.shape[0] * cap * cap)
    left, right = left_ops[0], right_ops[0]

    swap = [(i, i ^ 1) for i in range(sections)]
    other_h = lax.ppermute(source_h[0], "sect", swap)
    other_d = lax.ppermute(decay[0], "sect", swap)
    plan, own_psi, own_h, own_d, near_precond = start(
        slot_sector, pair_table, sector_sizes, ranks, psi_guess[0], source_h[0], decay[0], precond[0]
    )
    maps = chip_maps(own_h, other_h, own_d, other_d, chips)
    groups = [[2 * q + c for q in range(chips)] for c in range(2)]
    got_maps = lax.all_to_all(maps, "sect", 0, 0, tiled=True, axis_index_groups=groups)
    own_psi, late_precond, _ = lax.optimization_barrier((own_psi, near_precond, maps))
    got_psi = three(own_psi)
    own_half, half = half_message(late_precond)
    halves = three(own_half)
    got_maps, own_half = lax.optimization_barrier((got_maps, own_half))
    env = scan_maps(got_maps)
    got_env = lax.all_to_all(env, "sect", 0, 0, tiled=True, axis_index_groups=groups)
    env_own = got_env.reshape(slots // 2, cap, cap)
    psi, ops = first_products(plan, [own_psi] + got_psi, left, right)
    env_own, ops, halves[1:] = lax.optimization_barrier((env_own, ops, halves[1:]))
    env_got = lax.ppermute(env_own, "sect", swap)
    env_low, a_own, upper, lower = first_close(
        plan, psi, ops, env_own, env_got, other_h, other_d, half
    )
    lower, halves[0] = lax.optimization_barrier((lower, halves[0]))
    for step in range(1, STEPS):
        last = step == STEPS - 1
        later_left, later_right, _ = lax.optimization_barrier((left, right, lower))
        got, (far_b, later_left) = pass_on(
            upper, lower, functools.partial(ready_left, halves, psi, later_left)
        )
        later_right = ready_right(later_right)
        psi, a_own, *sent = later_step(
            plan, entries, a_own, lower, got, far_b, psi, env_low, half, later_left, later_right, last
        )
        upper, lower = sent[0], sent[-1]
    tile = lower
    near = near_message(a_own, psi, half)
    behind = [(i + 1, i) for i in range(sections - 1)]
    near = lax.ppermute(near, "sect", behind)
    factors, energies = settle([tile] + three(tile), entries)
    near_factors = lax.ppermute(factors, "sect", behind)
    ground, scaled = ground_state(plan, factors, a_own, psi, half, inv_sv[0])
    merged = merge(near_factors, scaled, near)
    return (ground[None], energies, merged[None])


def solution(mesh):
    in_specs = (
        P("sect", "blk", None, None),
        P("sect", None),
        P(),
        P(),
        P("sect", "blk", None, None, None),
        P("sect", "blk", None, None, None),
        P("sect", "blk", None),
        P("sect", "blk", None, None),
        P("sect", "blk", None, None),
        P("sect", "blk", None),
        P("sect", None),
    )
    out_specs = (P("sect", "blk", None, None), P("sect"), P("sect", "blk", None, None))
    return jax.shard_map(shards, mesh=mesh, in_specs=in_specs, out_specs=out_specs, check_vma=False)
```

```python
import functools

import jax
import jax.numpy as jnp
from jax import lax
from jax.experimental import pallas as pl
from jax.experimental.pallas import tpu as pltpu
from jax.sharding import PartitionSpec as P

STEPS = 3
DAMPING = 0.5
F32 = jnp.float32
BF16 = jnp.bfloat16
VMEM = pltpu.VMEM
SMEM = pltpu.SMEM
HBM = pltpu.HBM
LIMIT = 20 * 1024 * 1024
SIZES, RANKS, CORE, SOURCES = 0, 64, 96, 128


def params(**more):
    return pltpu.CompilerParams(vmem_limit_bytes=LIMIT, **more)


def whole(space=VMEM):
    return pl.BlockSpec(memory_space=space)


def in_hbm(value):
    return pltpu.with_memory_space_constraint(value, HBM)


def cost(flops, bytes_accessed):
    return pl.CostEstimate(flops=flops, bytes_accessed=bytes_accessed, transcendentals=0)


def start_kernel(
    slot_hbm,
    pair_hbm,
    sizes_hbm,
    ranks_hbm,
    psi_hbm,
    h_hbm,
    d_hbm,
    precond_hbm,
    plan,
    out_ref,
    h_ref,
    d_ref,
    precond_ref,
    slot_sector,
    pair_table,
    sizes,
    ranks,
    slot_of,
    psi_ref,
    sem,
):
    terms, sectors = pair_table.shape
    slots, cap, _ = out_ref.shape
    me = lax.axis_index("blk")
    core = lax.axis_index("sect") & 1
    moves = (
        (slot_hbm, slot_sector),
        (pair_hbm, pair_table),
        (sizes_hbm, sizes),
        (ranks_hbm, ranks),
        (psi_hbm, psi_ref),
        (d_hbm, d_ref),
        (h_hbm.at[pl.ds(core * (slots // 2), slots // 2)], h_ref),
        (precond_hbm, precond_ref),
    )
    fetches = [pltpu.make_async_copy(a, b, sem.at[k]) for k, (a, b) in enumerate(moves)]
    for fetch in fetches:
        fetch.start()
    for fetch in fetches[:5]:
        fetch.wait()
    plan[CORE] = core
    for j in range(slots):
        sector = slot_sector[me * slots + j]
        size = sizes[0, sector]
        plan[SIZES + j] = size
        plan[RANKS + j] = ranks[0, sector]
        block = jnp.where(support_of(size, cap), psi_ref[j].astype(F32), 0.0)
        out_ref[j] = block.astype(BF16)
    for slot in range(sectors):
        slot_of[slot_sector[slot]] = slot

    def tables(j, carry):
        sector = slot_sector[me * slots + j]
        for w in range(terms):
            source = slot_of[pair_table[w, sector]]
            plan[SOURCES + j * terms + w] = ((me * slots - (source & -slots)) & (3 * slots)) | (
                source & (slots - 1)
            )
        return carry

    lax.fori_loop(0, slots, tables, 0)
    for fetch in fetches[5:]:
        fetch.wait()


def start(slot_sector, pair_table, sizes, ranks, psi, own_h, own_d, precond):
    pairs = pair_table.T
    terms = pairs.shape[0]
    slots = psi.shape[0]
    tables = (slot_sector, pairs, sizes, ranks)
    return pl.pallas_call(
        start_kernel,
        out_shape=[
            jax.ShapeDtypeStruct((SOURCES + slots * terms,), jnp.int32),
            jax.ShapeDtypeStruct(psi.shape, BF16),
            jax.ShapeDtypeStruct((slots // 2, *psi.shape[1:]), F32),
            jax.ShapeDtypeStruct(own_d.shape, F32),
            pltpu.VMEM(precond.shape, F32),
        ],
        in_specs=[whole(HBM)] * 8,
        out_specs=[whole(SMEM), whole(), whole(), whole(), whole()],
        scratch_shapes=[pltpu.SMEM(t.shape, jnp.int32) for t in tables]
        + [
            pltpu.SMEM(slot_sector.shape, jnp.int32),
            pltpu.VMEM(psi.shape, BF16),
            pltpu.SemaphoreType.DMA((8,)),
        ],
        compiler_params=params(),
        cost_estimate=cost(4 * psi.size, 4 * psi.size),
        name="start",
    )(*[in_hbm(t) for t in (*tables, psi, own_h, own_d, precond)])


def half_kernel(precond_ref, out_ref, half_ref):
    for j in range(precond_ref.shape[0]):
        half = DAMPING / precond_ref[j]
        half_ref[j] = half
        out_ref[j] = half.astype(BF16)


def half_message(precond):
    slots, cap, _ = precond.shape
    return pl.pallas_call(
        half_kernel,
        out_shape=[
            jax.ShapeDtypeStruct((slots, cap, cap), BF16),
            jax.ShapeDtypeStruct((slots, cap, cap), F32),
        ],
        in_specs=[whole()],
        out_specs=[whole(), whole()],
        compiler_params=params(),
        cost_estimate=cost(2 * slots * cap * cap, 100 * slots * cap * cap),
        name="half_message",
    )(precond)


def chip_kernel(own_h, other_h, own_d, other_d, out_ref, late_t):
    slots, cap = own_d.shape
    mine = slots // 2
    chips, rows, _ = out_ref.shape
    chunk = rows - 8
    cuts = cap // chunk
    core_here = lax.axis_index("sect") & 1
    row = lax.broadcasted_iota(jnp.int32, (8, cap), 0)

    def emit(core):
        early_d, late_d = (own_d, other_d) if core == 0 else (other_d, own_d)
        late_t[...] = jnp.transpose(late_d[...])
        whole_d = early_d[...] * late_d[...]
        high = whole_d.astype(BF16).astype(F32)
        low = whole_d - high
        for j in range(mine):
            k = core * mine + j
            tail = jnp.where(
                row == 0, high[k : k + 1, :], jnp.where(row == 1, low[k : k + 1, :], 0.0)
            )
            early_h, late_h = (own_h[j], other_h[k]) if core == 0 else (other_h[k], own_h[j])
            both = late_t[:, k : k + 1] * early_h * late_d[k : k + 1, :] + late_h
            for cut in range(cuts):
                part = jnp.concatenate([both[cut * chunk : (cut + 1) * chunk], tail], axis=0)
                out_ref[j * cuts + cut] = part.astype(BF16)

    @pl.when(core_here == 0)
    def _():
        emit(0)

    @pl.when(core_here != 0)
    def _():
        emit(1)


def chip_maps(own_h, other_h, own_d, other_d, chips):
    slots, cap = own_d.shape
    chunk = slots // 2 * cap // chips
    return pl.pallas_call(
        chip_kernel,
        out_shape=jax.ShapeDtypeStruct((chips, chunk + 8, cap), BF16),
        in_specs=[whole()] * 4,
        out_specs=whole(),
        scratch_shapes=[pltpu.VMEM((cap, slots), F32)],
        compiler_params=params(),
        cost_estimate=cost(2 * slots * cap * cap, 6 * slots * cap * cap),
        name="chip_maps",
    )(own_h, other_h, own_d, other_d)


def scan_kernel(maps_ref, out_ref, factor, factor_t):
    chips, chunk, cap = out_ref.shape
    cuts = cap // chunk
    for z in range(chips):
        tail = maps_ref[z].astype(F32)[chunk : chunk + 8]
        factor[z : z + 1, :] = tail[0:1, :] + tail[1:2, :]
    factor_t[...] = jnp.transpose(factor[...])
    first = pl.multiple_of(lax.rem(lax.axis_index("sect") // 2, cuts) * chunk, chunk)
    columns = factor_t[pl.ds(first, chunk), :]
    state = jnp.zeros((chunk, cap), F32)
    for z in range(chips):
        out_ref[z] = state.astype(BF16)
        source = maps_ref[z].astype(F32)[0:chunk]
        state = columns[:, z : z + 1] * state * factor[z : z + 1, :] + source


def scan_maps(maps):
    chips, rows, cap = maps.shape
    chunk = rows - 8
    return pl.pallas_call(
        scan_kernel,
        out_shape=jax.ShapeDtypeStruct((chips, chunk, cap), BF16),
        in_specs=[whole()],
        out_specs=whole(),
        scratch_shapes=[pltpu.VMEM((chips, cap), F32), pltpu.VMEM((cap, chips), F32)],
        compiler_params=params(),
        cost_estimate=cost(4 * chips * chunk * cap, 200 * chips * chunk * cap),
        name="scan_maps",
    )(maps)


def pack_rows(values, cap):
    row = lax.broadcasted_iota(jnp.int32, (16, cap), 0)
    tile = jnp.zeros((16, cap), F32)
    for k, value in enumerate(values):
        rest = jnp.broadcast_to(value, (16, cap))
        for piece in range(3):
            part = rest.astype(BF16).astype(F32)
            tile = jnp.where(row == 3 * k + piece, part, tile)
            rest = rest - part
    return tile.astype(BF16)


def unpack_rows(tile, count):
    tile = tile.astype(F32)
    return [
        tile[3 * k : 3 * k + 1] + tile[3 * k + 1 : 3 * k + 2] + tile[3 * k + 2 : 3 * k + 3]
        for k in range(count)
    ]


def local_quotient(numerator, overlap):
    return jnp.where(overlap > 0.0, numerator / jnp.where(overlap > 0.0, overlap, 1.0), 0.0)


def paired(values):
    return (values[0] + values[2]) + (values[1] + values[3])


def resolve(tiles, entries):
    sums = [unpack_rows(tile, 5) for tile in tiles]
    rayleigh = paired([s[0] for s in sums]) / paired([s[1] for s in sums])
    deltas = [rayleigh - local_quotient(s[0], s[1]) for s in sums]
    squares = paired(
        [s[2] + delta * (2.0 * s[3] + delta * s[4]) for s, delta in zip(sums, deltas)]
    )
    scale = lax.rsqrt(squares / entries + 1e-06)
    return rayleigh, deltas, scale


def total(x):
    return jnp.sum(jnp.sum(x, axis=0, keepdims=True), axis=1, keepdims=True)


AHEAD = 3


def products(j, plan, left_ref, right_ref, psi_ref, inner):
    terms, cap = left_ref.shape[1], left_ref.shape[2]
    for w in range(terms):
        inner[:, w * cap : (w + 1) * cap] = jnp.dot(
            left_ref[j, w], psi_ref[plan[SOURCES + j * terms + w]], preferred_element_type=F32
        ).astype(BF16)
    result = jnp.zeros((cap, cap), F32)
    for w in range(0, terms, 2):
        pair = jnp.concatenate([right_ref[j, w], right_ref[j, w + 1]], axis=1)
        result = result + lax.dot_general(
            inner[:, w * cap : (w + 2) * cap],
            pair,
            (((1,), (1,)), ((), ())),
            preferred_element_type=F32,
        )
    return result


def support_of(size, cap):
    row = lax.broadcasted_iota(jnp.int32, (cap, cap), 0)
    column = lax.broadcasted_iota(jnp.int32, (cap, cap), 1)
    return (row < size) & (column < size)


def close_step(psi_ref, half_ref, applied, a_ref, upper_ref, lower_ref):
    slots, cap, _ = applied.shape
    zero = jnp.zeros((cap, cap), F32)
    numerator, overlap = zero, zero
    for j in range(slots):
        current = psi_ref[j].astype(F32)
        numerator = numerator + current * applied[j]
        overlap = overlap + current * current
    numerator, overlap = total(numerator), total(overlap)
    quotient = local_quotient(numerator, overlap)
    aa, ab, bb = zero, zero, zero
    for j in range(slots):
        current = psi_ref[j].astype(F32)
        half = half_ref[j]
        a = current - half * (applied[j] - quotient * current)
        b = half * current
        a_ref[j] = a
        if upper_ref is None:
            pass
        elif j < slots // 2:
            upper_ref[j * cap : (j + 1) * cap, :] = a.astype(BF16)
        else:
            i = j - slots // 2
            lower_ref[i * cap : (i + 1) * cap, :] = a.astype(BF16)
        aa = aa + a * a
        ab = ab + a * b
        bb = bb + b * b
    sums = [numerator, overlap, total(aa), total(ab), total(bb)]
    rows = lower_ref.shape[0]
    lower_ref[rows - 16 : rows, :] = pack_rows(sums, cap)


def first_kernel(
    plan,
    psi_0,
    psi_1,
    psi_2,
    psi_3,
    left_hbm,
    right_hbm,
    psi_ref,
    ops_ref,
    inner,
    left_ref,
    right_ref,
    psi_sem,
    ops_sem,
):
    slots = psi_0.shape[0]
    fetches = []
    for k, part in enumerate((psi_0, psi_1, psi_2, psi_3)):
        target = psi_ref.at[pl.ds(k * slots, slots)]
        fetches.append(pltpu.make_async_copy(part, target, psi_sem.at[k]))

    def fetch_ops(j):
        return (
            pltpu.make_async_copy(left_hbm.at[j], left_ref.at[j], ops_sem.at[0, j]),
            pltpu.make_async_copy(right_hbm.at[j], right_ref.at[j], ops_sem.at[1, j]),
        )

    def begin(j):
        for copy in fetch_ops(j):
            copy.start()

    for fetch in fetches:
        fetch.start()
    begin(0)
    for fetch in fetches:
        fetch.wait()
    for j in range(1, AHEAD):
        begin(j)

    def one(j, carry):
        for copy in fetch_ops(j):
            copy.wait()

        @pl.when(j + AHEAD < slots)
        def _():
            begin(j + AHEAD)

        ops_ref[j] = products(j, plan, left_ref, right_ref, psi_ref, inner)
        return carry

    lax.fori_loop(0, slots, one, 0)


def close_kernel(
    plan,
    psi_ref,
    ops_ref,
    env_own,
    env_got,
    other_h,
    other_d,
    half_ref,
    env_low,
    a_ref,
    upper_ref,
    lower_ref,
    applied,
    other_t,
):
    slots, cap = applied.shape[0], applied.shape[1]
    core = plan[CORE]
    other_t[...] = jnp.transpose(other_d[...])
    for j in range(slots):
        mine = slots // 2
        own, got = env_own[j % mine], env_got[j % mine]
        env = jnp.where(core == j // mine, own.astype(F32), got.astype(F32))
        further = other_t[:, j : j + 1] * env * other_d[j : j + 1, :] + other_h[j]
        env = jnp.where(core == 0, env, further).astype(BF16)
        env_low[j] = env
        result = ops_ref[j] + jnp.dot(env, psi_ref[j], preferred_element_type=F32)
        applied[j] = jnp.where(support_of(plan[SIZES + j], cap), result, 0.0)
    close_step(psi_ref, half_ref, applied, a_ref, upper_ref, lower_ref)


def later_kernel(
    last,
    entries,
    plan,
    a_own,
    lower_0,
    upper_1,
    lower_1,
    upper_2,
    lower_2,
    upper_3,
    lower_3,
    far_b,
    before,
    env_low,
    half_ref,
    left_ref,
    right_ref,
    psi_ref,
    a_ref,
    *more,
):
    upper_ref = None if last else more[0]
    lower_ref, applied, inner = more[-3:]
    slots, cap = applied.shape[0], applied.shape[1]
    rows = lower_1.shape[0]
    tiles = [m[rows - 16 : rows, :] for m in (lower_0, lower_1, lower_2, lower_3)]
    _, deltas, scale = resolve(tiles, entries)
    for i in range(slots):
        b = half_ref[i] * before[i].astype(F32)
        psi_ref[i] = (scale * (a_own[i] + deltas[0] * b)).astype(BF16)
    received = ((upper_1, lower_1), (upper_2, lower_2), (upper_3, lower_3))
    for k, (upper, lower) in enumerate(received, 1):
        for i in range(slots):
            message, at = (upper, i) if i < slots // 2 else (lower, i - slots // 2)
            a = message[at * cap : (at + 1) * cap, :].astype(F32)
            b = far_b[(k - 1) * slots + i].astype(F32)
            psi_ref[k * slots + i] = (scale * (a + deltas[k] * b)).astype(BF16)

    def one(j, carry):
        result = products(j, plan, left_ref, right_ref, psi_ref, inner)
        result = result + jnp.dot(env_low[j], psi_ref[j], preferred_element_type=F32)
        applied[j] = jnp.where(support_of(plan[SIZES + j], cap), result, 0.0)
        return carry

    lax.fori_loop(0, slots, one, 0, unroll=True)
    close_step(psi_ref, half_ref, applied, a_ref, upper_ref, lower_ref)


def step_cost(left):
    slots, terms, cap, _ = left.shape
    return cost(4 * slots * terms * cap**3, 12 * slots * terms * cap * cap)


def first_products(plan, psi, left, right):
    slots, terms, cap, _ = left.shape
    return pl.pallas_call(
        first_kernel,
        out_shape=[
            jax.ShapeDtypeStruct((4 * slots, cap, cap), BF16),
            jax.ShapeDtypeStruct((slots, cap, cap), F32),
        ],
        in_specs=[whole(SMEM)] + [whole(HBM)] * 6,
        out_specs=[whole()] * 2,
        scratch_shapes=[
            pltpu.VMEM((cap, terms * cap), BF16),
            pltpu.VMEM(left.shape, BF16),
            pltpu.VMEM(right.shape, BF16),
            pltpu.SemaphoreType.DMA((4,)),
            pltpu.SemaphoreType.DMA((2, slots)),
        ],
        compiler_params=params(),
        cost_estimate=cost(cap**3, slots * cap * cap),
        name="first_products",
    )(plan, *[in_hbm(p) for p in psi], in_hbm(left), in_hbm(right))


def ready_kernel(half_1, half_2, half_3, before, left_hbm, b_ref, left_ref, sem):
    slots = half_1.shape[0]
    left_copy = pltpu.make_async_copy(left_hbm, left_ref, sem)
    left_copy.start()
    for k, half in enumerate((half_1, half_2, half_3)):
        for i in range(slots):
            place = (k + 1) * slots + i
            b_ref[k * slots + i] = (half[i].astype(F32) * before[place].astype(F32)).astype(BF16)
    left_copy.wait()


def ready_left(halves, before, left):
    slots, _, cap, _ = left.shape
    return pl.pallas_call(
        ready_kernel,
        out_shape=[
            jax.ShapeDtypeStruct((3 * slots, cap, cap), BF16),
            pltpu.VMEM(left.shape, BF16),
        ],
        in_specs=[whole()] * 4 + [whole(HBM)],
        out_specs=[whole()] * 2,
        scratch_shapes=[pltpu.SemaphoreType.DMA],
        compiler_params=params(),
        cost_estimate=cost(3 * slots * cap * cap, 2 * left.size),
        name="ready_left",
    )(*halves, before, in_hbm(left))


def copy_kernel(right_hbm, right_ref, sem):
    right_copy = pltpu.make_async_copy(right_hbm, right_ref, sem)
    right_copy.start()
    right_copy.wait()


def ready_right(right):
    return pl.pallas_call(
        copy_kernel,
        out_shape=pltpu.VMEM(right.shape, BF16),
        in_specs=[whole(HBM)],
        out_specs=whole(),
        scratch_shapes=[pltpu.SemaphoreType.DMA],
        compiler_params=params(),
        cost_estimate=cost(right.size, 2 * right.size),
        name="ready_right",
    )(in_hbm(right))


def first_close(plan, psi, ops, env_own, env_got, other_h, other_d, half):
    slots, cap, _ = half.shape
    return pl.pallas_call(
        close_kernel,
        out_shape=[
            jax.ShapeDtypeStruct((slots, cap, cap), BF16),
            jax.ShapeDtypeStruct((slots, cap, cap), F32),
            jax.ShapeDtypeStruct((slots // 2 * cap, cap), BF16),
            jax.ShapeDtypeStruct((slots // 2 * cap + 16, cap), BF16),
        ],
        in_specs=[whole(SMEM)] + [whole()] * 7,
        out_specs=[whole()] * 4,
        scratch_shapes=[
            pltpu.VMEM((slots, cap, cap), F32),
            pltpu.VMEM((cap, slots), F32),
        ],
        compiler_params=params(),
        cost_estimate=cost(2 * slots * cap**3, 20 * slots * cap * cap),
        name="first_close",
    )(plan, psi, ops, env_own, env_got, other_h, other_d, half)


def later_step(plan, entries, a_own, lower, got, far_b, before, env, half, left, right, last):
    slots, terms, cap, _ = left.shape
    rows = slots // 2 * cap
    sent = [jax.ShapeDtypeStruct((16 if last else rows + 16, cap), BF16)]
    if not last:
        sent = [jax.ShapeDtypeStruct((rows, cap), BF16)] + sent
    return pl.pallas_call(
        functools.partial(later_kernel, last, entries),
        out_shape=[
            jax.ShapeDtypeStruct((4 * slots, cap, cap), BF16),
            jax.ShapeDtypeStruct((slots, cap, cap), F32),
            *sent,
        ],
        in_specs=[whole(SMEM)] + [whole()] * 14,
        out_specs=[whole()] * (2 + len(sent)),
        scratch_shapes=[
            pltpu.VMEM((slots, cap, cap), F32),
            pltpu.VMEM((cap, terms * cap), BF16),
        ],
        compiler_params=params(),
        cost_estimate=step_cost(left),
        name="last_step" if last else "later_step",
    )(plan, a_own, lower, *got, far_b, before, env, half, left, right)


def near_kernel(a_ref, psi_ref, half_ref, near_ref):
    for j in range(a_ref.shape[0]):
        near_ref[0, j] = a_ref[j].astype(BF16)
        near_ref[1, j] = (half_ref[j] * psi_ref[j].astype(F32)).astype(BF16)


def near_message(a_own, psi, half):
    slots, cap, _ = a_own.shape
    return pl.pallas_call(
        near_kernel,
        out_shape=jax.ShapeDtypeStruct((2, slots, cap, cap), BF16),
        in_specs=[whole()] * 3,
        out_specs=whole(),
        compiler_params=params(),
        cost_estimate=cost(2 * slots * cap * cap, 12 * slots * cap * cap),
        name="near_message",
    )(a_own, psi, half)


def settle_kernel(entries, tile_0, tile_1, tile_2, tile_3, factors_ref, energy_ref):
    tiles = [t[...] for t in (tile_0, tile_1, tile_2, tile_3)]
    rayleigh, deltas, scale = resolve(tiles, entries)
    energy_ref[0] = rayleigh[0, 0]
    factors_ref[...] = pack_rows([scale, deltas[0]], factors_ref.shape[1])


def settle(tiles, entries):
    cap = tiles[0].shape[1]
    return pl.pallas_call(
        functools.partial(settle_kernel, entries),
        out_shape=[jax.ShapeDtypeStruct((16, cap), BF16), jax.ShapeDtypeStruct((1,), F32)],
        in_specs=[whole()] * 4,
        out_specs=[whole(), whole(SMEM)],
        compiler_params=params(),
        cost_estimate=cost(16 * cap, 128 * cap),
        name="settle",
    )(*tiles)


def ground_kernel(plan, factors_ref, a_ref, psi_ref, half_ref, inv_sv, ground_ref, scaled_ref):
    slots, cap = a_ref.shape[0], a_ref.shape[1]
    scale, delta = unpack_rows(factors_ref[...], 2)
    lane = lax.broadcasted_iota(jnp.int32, (1, cap), 1)
    for j in range(slots):
        b = half_ref[j] * psi_ref[j].astype(F32)
        ground = (scale * (a_ref[j] + delta * b)).astype(BF16)
        ground_ref[j] = ground
        weight = jnp.where(lane < plan[RANKS + j], inv_sv[j : j + 1, :] / cap, 0.0)
        scaled_ref[j] = (ground.astype(F32) * weight).astype(BF16)


def ground_state(plan, factors, a_own, psi, half, inv_sv):
    slots, cap, _ = a_own.shape
    return pl.pallas_call(
        ground_kernel,
        out_shape=[jax.ShapeDtypeStruct((slots, cap, cap), BF16)] * 2,
        in_specs=[whole(SMEM)] + [whole()] * 5,
        out_specs=[whole(), whole()],
        compiler_params=params(),
        cost_estimate=cost(4 * slots * cap * cap, 12 * slots * cap * cap),
        name="ground_state",
    )(plan, factors, a_own, psi, half, inv_sv)


def merge_kernel(factors_ref, scaled_ref, near_ref, out_ref):
    live = lax.axis_index("sect") < lax.axis_size("sect") - 1
    scale, delta = unpack_rows(factors_ref[...], 2)
    for j in range(scaled_ref.shape[0]):
        following = scale * (near_ref[0, j].astype(F32) + delta * near_ref[1, j].astype(F32))
        merged = jnp.dot(scaled_ref[j], following.astype(BF16), preferred_element_type=F32)
        out_ref[j] = jnp.where(live, merged, 0.0).astype(BF16)


def merge(factors, scaled, near):
    slots, cap, _ = scaled.shape
    return pl.pallas_call(
        merge_kernel,
        out_shape=jax.ShapeDtypeStruct((slots, cap, cap), BF16),
        in_specs=[whole()] * 3,
        out_specs=whole(),
        compiler_params=params(),
        cost_estimate=cost(2 * slots * cap**3, 6 * slots * cap * cap),
        name="merge",
    )(factors, scaled, near)


def around(value, shift):
    count = lax.axis_size("blk")
    return lax.ppermute(value, "blk", [(i, (i + shift) % count) for i in range(count)])


def three(value):
    return [around(value, shift) for shift in (1, 2, 3)]


def pass_on(upper, lower, beside):
    upper_1 = around(upper, 1)
    lower_3 = around(lower, 3)
    lower_1 = around(lower, 1)
    upper_3 = around(upper, 3)
    done = list(beside())
    lower_3, done[0] = lax.optimization_barrier((lower_3, done[0]))
    upper_1, upper_3 = lax.optimization_barrier((upper_1, upper_3))
    upper_2 = around(upper_1, 1)
    lower_2 = around(lower_3, 3)
    return [upper_1, lower_1, upper_2, lower_2, upper_3, lower_3], done


def shards(
    psi_guess,
    sector_sizes,
    slot_sector,
    pair_table,
    left_ops,
    right_ops,
    decay,
    source_h,
    precond,
    inv_sv,
    ranks,
):
    sections = lax.axis_size("sect")
    chips = sections // 2
    slots, cap = psi_guess.shape[1], psi_guess.shape[2]
    entries = float(slot_sector.shape[0] * cap * cap)
    left, right = left_ops[0], right_ops[0]

    swap = [(i, i ^ 1) for i in range(sections)]
    other_h = lax.ppermute(source_h[0], "sect", swap)
    other_d = lax.ppermute(decay[0], "sect", swap)
    plan, own_psi, own_h, own_d, near_precond = start(
        slot_sector, pair_table, sector_sizes, ranks, psi_guess[0], source_h[0], decay[0], precond[0]
    )
    maps = chip_maps(own_h, other_h, own_d, other_d, chips)
    groups = [[2 * q + c for q in range(chips)] for c in range(2)]
    got_maps = lax.all_to_all(maps, "sect", 0, 0, tiled=True, axis_index_groups=groups)
    own_psi, late_precond, _ = lax.optimization_barrier((own_psi, near_precond, maps))
    got_psi = three(own_psi)
    own_half, half = half_message(late_precond)
    halves = three(own_half)
    got_maps, own_half = lax.optimization_barrier((got_maps, own_half))
    env = scan_maps(got_maps)
    got_env = lax.all_to_all(env, "sect", 0, 0, tiled=True, axis_index_groups=groups)
    env_own = got_env.reshape(slots // 2, cap, cap)
    psi, ops = first_products(plan, [own_psi] + got_psi, left, right)
    env_own, ops, halves[1:] = lax.optimization_barrier((env_own, ops, halves[1:]))
    env_got = lax.ppermute(env_own, "sect", swap)
    env_low, a_own, upper, lower = first_close(
        plan, psi, ops, env_own, env_got, other_h, other_d, half
    )
    lower, halves[0] = lax.optimization_barrier((lower, halves[0]))
    for step in range(1, STEPS):
        last = step == STEPS - 1
        later_left, later_right, _ = lax.optimization_barrier((left, right, lower))
        got, (far_b, later_left) = pass_on(
            upper, lower, functools.partial(ready_left, halves, psi, later_left)
        )
        later_right = ready_right(later_right)
        psi, a_own, *sent = later_step(
            plan, entries, a_own, lower, got, far_b, psi, env_low, half, later_left, later_right, last
        )
        upper, lower = sent[0], sent[-1]
    tile = lower
    near = near_message(a_own, psi, half)
    behind = [(i + 1, i) for i in range(sections - 1)]
    near = lax.ppermute(near, "sect", behind)
    factors, energies = settle([tile] + three(tile), entries)
    near_factors = lax.ppermute(factors, "sect", behind)
    ground, scaled = ground_state(plan, factors, a_own, psi, half, inv_sv[0])
    merged = merge(near_factors, scaled, near)
    return (ground[None], energies, merged[None])


def solution(mesh):
    in_specs = (
        P("sect", "blk", None, None),
        P("sect", None),
        P(),
        P(),
        P("sect", "blk", None, None, None),
        P("sect", "blk", None, None, None),
        P("sect", "blk", None),
        P("sect", "blk", None, None),
        P("sect", "blk", None, None),
        P("sect", "blk", None),
        P("sect", None),
    )
    out_specs = (P("sect", "blk", None, None), P("sect"), P("sect", "blk", None, None))
    return jax.shard_map(shards, mesh=mesh, in_specs=in_specs, out_specs=out_specs, check_vma=False)
```

```python
import functools

import jax
import jax.numpy as jnp
from jax import lax
from jax.experimental import pallas as pl
from jax.experimental.pallas import tpu as pltpu
from jax.sharding import PartitionSpec as P

STEPS = 3
DAMPING = 0.5
F32 = jnp.float32
BF16 = jnp.bfloat16
VMEM = pltpu.VMEM
SMEM = pltpu.SMEM
HBM = pltpu.HBM
LIMIT = 20 * 1024 * 1024
SIZES, RANKS, CORE, SOURCES = 0, 64, 96, 128


def params(**more):
    return pltpu.CompilerParams(vmem_limit_bytes=LIMIT, **more)


def whole(space=VMEM):
    return pl.BlockSpec(memory_space=space)


def in_hbm(value):
    return pltpu.with_memory_space_constraint(value, HBM)


def cost(flops, bytes_accessed):
    return pl.CostEstimate(flops=flops, bytes_accessed=bytes_accessed, transcendentals=0)


def start_kernel(
    slot_hbm,
    pair_hbm,
    sizes_hbm,
    ranks_hbm,
    psi_hbm,
    h_hbm,
    d_hbm,
    precond_hbm,
    plan,
    out_ref,
    h_ref,
    d_ref,
    precond_ref,
    slot_sector,
    pair_table,
    sizes,
    ranks,
    slot_of,
    psi_ref,
    sem,
):
    terms, sectors = pair_table.shape
    slots, cap, _ = out_ref.shape
    me = lax.axis_index("blk")
    core = lax.axis_index("sect") & 1
    moves = (
        (slot_hbm, slot_sector),
        (pair_hbm, pair_table),
        (sizes_hbm, sizes),
        (ranks_hbm, ranks),
        (psi_hbm, psi_ref),
        (d_hbm, d_ref),
        (h_hbm.at[pl.ds(core * (slots // 2), slots // 2)], h_ref),
        (precond_hbm, precond_ref),
    )
    fetches = [pltpu.make_async_copy(a, b, sem.at[k]) for k, (a, b) in enumerate(moves)]
    for fetch in fetches:
        fetch.start()
    for fetch in fetches[:5]:
        fetch.wait()
    plan[CORE] = core
    for j in range(slots):
        sector = slot_sector[me * slots + j]
        size = sizes[0, sector]
        plan[SIZES + j] = size
        plan[RANKS + j] = ranks[0, sector]
        block = jnp.where(support_of(size, cap), psi_ref[j].astype(F32), 0.0)
        out_ref[j] = block.astype(BF16)
    for slot in range(sectors):
        slot_of[slot_sector[slot]] = slot

    def tables(j, carry):
        sector = slot_sector[me * slots + j]
        for w in range(terms):
            source = slot_of[pair_table[w, sector]]
            plan[SOURCES + j * terms + w] = ((me * slots - (source & -slots)) & (3 * slots)) | (
                source & (slots - 1)
            )
        return carry

    lax.fori_loop(0, slots, tables, 0)
    for fetch in fetches[5:]:
        fetch.wait()


def start(slot_sector, pair_table, sizes, ranks, psi, own_h, own_d, precond):
    pairs = pair_table.T
    terms = pairs.shape[0]
    slots = psi.shape[0]
    tables = (slot_sector, pairs, sizes, ranks)
    return pl.pallas_call(
        start_kernel,
        out_shape=[
            jax.ShapeDtypeStruct((SOURCES + slots * terms,), jnp.int32),
            jax.ShapeDtypeStruct(psi.shape, BF16),
            jax.ShapeDtypeStruct((slots // 2, *psi.shape[1:]), F32),
            jax.ShapeDtypeStruct(own_d.shape, F32),
            pltpu.VMEM(precond.shape, F32),
        ],
        in_specs=[whole(HBM)] * 8,
        out_specs=[whole(SMEM), whole(), whole(), whole(), whole()],
        scratch_shapes=[pltpu.SMEM(t.shape, jnp.int32) for t in tables]
        + [
            pltpu.SMEM(slot_sector.shape, jnp.int32),
            pltpu.VMEM(psi.shape, BF16),
            pltpu.SemaphoreType.DMA((8,)),
        ],
        compiler_params=params(),
        cost_estimate=cost(4 * psi.size, 4 * psi.size),
        name="start",
    )(*[in_hbm(t) for t in (*tables, psi, own_h, own_d, precond)])


def half_kernel(precond_ref, out_ref, half_ref):
    for j in range(precond_ref.shape[0]):
        half = DAMPING / precond_ref[j]
        half_ref[j] = half
        out_ref[j] = half.astype(BF16)


def half_message(precond):
    slots, cap, _ = precond.shape
    return pl.pallas_call(
        half_kernel,
        out_shape=[
            jax.ShapeDtypeStruct((slots, cap, cap), BF16),
            jax.ShapeDtypeStruct((slots, cap, cap), F32),
        ],
        in_specs=[whole()],
        out_specs=[whole(), whole()],
        compiler_params=params(),
        cost_estimate=cost(2 * slots * cap * cap, 100 * slots * cap * cap),
        name="half_message",
    )(precond)


def chip_kernel(own_h, other_h, own_d, other_d, out_ref, late_t):
    slots, cap = own_d.shape
    mine = slots // 2
    chips, rows, _ = out_ref.shape
    chunk = rows - 8
    cuts = cap // chunk
    core_here = lax.axis_index("sect") & 1
    row = lax.broadcasted_iota(jnp.int32, (8, cap), 0)

    def emit(core):
        early_d, late_d = (own_d, other_d) if core == 0 else (other_d, own_d)
        late_t[...] = jnp.transpose(late_d[...])
        whole_d = early_d[...] * late_d[...]
        high = whole_d.astype(BF16).astype(F32)
        low = whole_d - high
        for j in range(mine):
            k = core * mine + j
            tail = jnp.where(
                row == 0, high[k : k + 1, :], jnp.where(row == 1, low[k : k + 1, :], 0.0)
            )
            early_h, late_h = (own_h[j], other_h[k]) if core == 0 else (other_h[k], own_h[j])
            both = late_t[:, k : k + 1] * early_h * late_d[k : k + 1, :] + late_h
            for cut in range(cuts):
                part = jnp.concatenate([both[cut * chunk : (cut + 1) * chunk], tail], axis=0)
                out_ref[j * cuts + cut] = part.astype(BF16)

    @pl.when(core_here == 0)
    def _():
        emit(0)

    @pl.when(core_here != 0)
    def _():
        emit(1)


def chip_maps(own_h, other_h, own_d, other_d, chips):
    slots, cap = own_d.shape
    chunk = slots // 2 * cap // chips
    return pl.pallas_call(
        chip_kernel,
        out_shape=jax.ShapeDtypeStruct((chips, chunk + 8, cap), BF16),
        in_specs=[whole()] * 4,
        out_specs=whole(),
        scratch_shapes=[pltpu.VMEM((cap, slots), F32)],
        compiler_params=params(),
        cost_estimate=cost(2 * slots * cap * cap, 6 * slots * cap * cap),
        name="chip_maps",
    )(own_h, other_h, own_d, other_d)


def scan_kernel(maps_ref, out_ref, factor, factor_t):
    chips, chunk, cap = out_ref.shape
    cuts = cap // chunk
    for z in range(chips):
        tail = maps_ref[z].astype(F32)[chunk : chunk + 8]
        factor[z : z + 1, :] = tail[0:1, :] + tail[1:2, :]
    factor_t[...] = jnp.transpose(factor[...])
    first = pl.multiple_of(lax.rem(lax.axis_index("sect") // 2, cuts) * chunk, chunk)
    columns = factor_t[pl.ds(first, chunk), :]
    state = jnp.zeros((chunk, cap), F32)
    for z in range(chips):
        out_ref[z] = state.astype(BF16)
        source = maps_ref[z].astype(F32)[0:chunk]
        state = columns[:, z : z + 1] * state * factor[z : z + 1, :] + source


def scan_maps(maps):
    chips, rows, cap = maps.shape
    chunk = rows - 8
    return pl.pallas_call(
        scan_kernel,
        out_shape=jax.ShapeDtypeStruct((chips, chunk, cap), BF16),
        in_specs=[whole()],
        out_specs=whole(),
        scratch_shapes=[pltpu.VMEM((chips, cap), F32), pltpu.VMEM((cap, chips), F32)],
        compiler_params=params(),
        cost_estimate=cost(4 * chips * chunk * cap, 200 * chips * chunk * cap),
        name="scan_maps",
    )(maps)


def pack_rows(values, cap):
    row = lax.broadcasted_iota(jnp.int32, (16, cap), 0)
    tile = jnp.zeros((16, cap), F32)
    for k, value in enumerate(values):
        rest = jnp.broadcast_to(value, (16, cap))
        for piece in range(3):
            part = rest.astype(BF16).astype(F32)
            tile = jnp.where(row == 3 * k + piece, part, tile)
            rest = rest - part
    return tile.astype(BF16)


def unpack_rows(tile, count):
    tile = tile.astype(F32)
    return [
        tile[3 * k : 3 * k + 1] + tile[3 * k + 1 : 3 * k + 2] + tile[3 * k + 2 : 3 * k + 3]
        for k in range(count)
    ]


def local_quotient(numerator, overlap):
    return jnp.where(overlap > 0.0, numerator / jnp.where(overlap > 0.0, overlap, 1.0), 0.0)


def paired(values):
    return (values[0] + values[2]) + (values[1] + values[3])


def resolve(tiles, entries):
    sums = [unpack_rows(tile, 5) for tile in tiles]
    rayleigh = paired([s[0] for s in sums]) / paired([s[1] for s in sums])
    deltas = [rayleigh - local_quotient(s[0], s[1]) for s in sums]
    squares = paired(
        [s[2] + delta * (2.0 * s[3] + delta * s[4]) for s, delta in zip(sums, deltas)]
    )
    scale = lax.rsqrt(squares / entries + 1e-06)
    return rayleigh, deltas, scale


def total(x):
    return jnp.sum(jnp.sum(x, axis=0, keepdims=True), axis=1, keepdims=True)


AHEAD = 4


def products(j, plan, left_ref, right_ref, psi_ref, inner):
    terms, cap = left_ref.shape[1], left_ref.shape[2]
    for w in range(terms):
        inner[:, w * cap : (w + 1) * cap] = jnp.dot(
            left_ref[j, w], psi_ref[plan[SOURCES + j * terms + w]], preferred_element_type=F32
        ).astype(BF16)
    result = jnp.zeros((cap, cap), F32)
    for w in range(0, terms, 2):
        pair = jnp.concatenate([right_ref[j, w], right_ref[j, w + 1]], axis=1)
        result = result + lax.dot_general(
            inner[:, w * cap : (w + 2) * cap],
            pair,
            (((1,), (1,)), ((), ())),
            preferred_element_type=F32,
        )
    return result


def support_of(size, cap):
    row = lax.broadcasted_iota(jnp.int32, (cap, cap), 0)
    column = lax.broadcasted_iota(jnp.int32, (cap, cap), 1)
    return (row < size) & (column < size)


def close_step(psi_ref, half_ref, applied, a_ref, upper_ref, lower_ref):
    slots, cap, _ = applied.shape
    zero = jnp.zeros((cap, cap), F32)
    numerator, overlap = zero, zero
    for j in range(slots):
        current = psi_ref[j].astype(F32)
        numerator = numerator + current * applied[j]
        overlap = overlap + current * current
    numerator, overlap = total(numerator), total(overlap)
    quotient = local_quotient(numerator, overlap)
    aa, ab, bb = zero, zero, zero
    for j in range(slots):
        current = psi_ref[j].astype(F32)
        half = half_ref[j]
        a = current - half * (applied[j] - quotient * current)
        b = half * current
        a_ref[j] = a
        if upper_ref is None:
            pass
        elif j < slots // 2:
            upper_ref[j * cap : (j + 1) * cap, :] = a.astype(BF16)
        else:
            i = j - slots // 2
            lower_ref[i * cap : (i + 1) * cap, :] = a.astype(BF16)
        aa = aa + a * a
        ab = ab + a * b
        bb = bb + b * b
    sums = [numerator, overlap, total(aa), total(ab), total(bb)]
    rows = lower_ref.shape[0]
    lower_ref[rows - 16 : rows, :] = pack_rows(sums, cap)


def first_kernel(
    plan,
    psi_0,
    psi_1,
    psi_2,
    psi_3,
    left_hbm,
    right_hbm,
    psi_ref,
    ops_ref,
    inner,
    left_ref,
    right_ref,
    psi_sem,
    ops_sem,
):
    slots = psi_0.shape[0]
    fetches = []
    for k, part in enumerate((psi_0, psi_1, psi_2, psi_3)):
        target = psi_ref.at[pl.ds(k * slots, slots)]
        fetches.append(pltpu.make_async_copy(part, target, psi_sem.at[k]))

    def fetch_ops(j):
        return (
            pltpu.make_async_copy(left_hbm.at[j], left_ref.at[j], ops_sem.at[0, j]),
            pltpu.make_async_copy(right_hbm.at[j], right_ref.at[j], ops_sem.at[1, j]),
        )

    def begin(j):
        for copy in fetch_ops(j):
            copy.start()

    for fetch in fetches:
        fetch.start()
    begin(0)
    for fetch in fetches:
        fetch.wait()
    for j in range(1, AHEAD):
        begin(j)

    def arrive(j):
        for copy in fetch_ops(j):
            copy.wait()

    def some(first):
        for j in range(first, first + AHEAD):
            ops_ref[j] = products(j, plan, left_ref, right_ref, psi_ref, inner)

    for j in range(AHEAD):
        arrive(j)
        begin(AHEAD + j)
    some(0)
    for j in range(AHEAD):
        arrive(AHEAD + j)
    some(AHEAD)


def close_kernel(
    plan,
    psi_ref,
    ops_ref,
    env_own,
    env_got,
    other_h,
    other_d,
    half_ref,
    env_low,
    a_ref,
    upper_ref,
    lower_ref,
    applied,
    other_t,
):
    slots, cap = applied.shape[0], applied.shape[1]
    core = plan[CORE]
    other_t[...] = jnp.transpose(other_d[...])
    for j in range(slots):
        mine = slots // 2
        own, got = env_own[j % mine], env_got[j % mine]
        env = jnp.where(core == j // mine, own.astype(F32), got.astype(F32))
        further = other_t[:, j : j + 1] * env * other_d[j : j + 1, :] + other_h[j]
        env = jnp.where(core == 0, env, further).astype(BF16)
        env_low[j] = env
        result = ops_ref[j] + jnp.dot(env, psi_ref[j], preferred_element_type=F32)
        applied[j] = jnp.where(support_of(plan[SIZES + j], cap), result, 0.0)
    close_step(psi_ref, half_ref, applied, a_ref, upper_ref, lower_ref)


def later_kernel(
    last,
    entries,
    plan,
    a_own,
    lower_0,
    upper_1,
    lower_1,
    upper_2,
    lower_2,
    upper_3,
    lower_3,
    far_b,
    before,
    env_low,
    half_ref,
    left_ref,
    right_ref,
    psi_ref,
    a_ref,
    *more,
):
    upper_ref = None if last else more[0]
    lower_ref, applied, inner = more[-3:]
    slots, cap = applied.shape[0], applied.shape[1]
    rows = lower_1.shape[0]
    tiles = [m[rows - 16 : rows, :] for m in (lower_0, lower_1, lower_2, lower_3)]
    _, deltas, scale = resolve(tiles, entries)
    for i in range(slots):
        b = half_ref[i] * before[i].astype(F32)
        psi_ref[i] = (scale * (a_own[i] + deltas[0] * b)).astype(BF16)
    received = ((upper_1, lower_1), (upper_2, lower_2), (upper_3, lower_3))
    for k, (upper, lower) in enumerate(received, 1):
        for i in range(slots):
            message, at = (upper, i) if i < slots // 2 else (lower, i - slots // 2)
            a = message[at * cap : (at + 1) * cap, :].astype(F32)
            b = far_b[(k - 1) * slots + i].astype(F32)
            psi_ref[k * slots + i] = (scale * (a + deltas[k] * b)).astype(BF16)

    def one(j, carry):
        result = products(j, plan, left_ref, right_ref, psi_ref, inner)
        result = result + jnp.dot(env_low[j], psi_ref[j], preferred_element_type=F32)
        applied[j] = jnp.where(support_of(plan[SIZES + j], cap), result, 0.0)
        return carry

    lax.fori_loop(0, slots, one, 0, unroll=True)
    close_step(psi_ref, half_ref, applied, a_ref, upper_ref, lower_ref)


def step_cost(left):
    slots, terms, cap, _ = left.shape
    return cost(4 * slots * terms * cap**3, 12 * slots * terms * cap * cap)


def first_products(plan, psi, left, right):
    slots, terms, cap, _ = left.shape
    return pl.pallas_call(
        first_kernel,
        out_shape=[
            jax.ShapeDtypeStruct((4 * slots, cap, cap), BF16),
            jax.ShapeDtypeStruct((slots, cap, cap), F32),
        ],
        in_specs=[whole(SMEM)] + [whole(HBM)] * 6,
        out_specs=[whole()] * 2,
        scratch_shapes=[
            pltpu.VMEM((cap, terms * cap), BF16),
            pltpu.VMEM(left.shape, BF16),
            pltpu.VMEM(right.shape, BF16),
            pltpu.SemaphoreType.DMA((4,)),
            pltpu.SemaphoreType.DMA((2, slots)),
        ],
        compiler_params=params(),
        cost_estimate=cost(cap**3, slots * cap * cap),
        name="first_products",
    )(plan, *[in_hbm(p) for p in psi], in_hbm(left), in_hbm(right))


def ready_kernel(half_1, half_2, half_3, before, left_hbm, b_ref, left_ref, sem):
    slots = half_1.shape[0]
    left_copy = pltpu.make_async_copy(left_hbm, left_ref, sem)
    left_copy.start()
    for k, half in enumerate((half_1, half_2, half_3)):
        for i in range(slots):
            place = (k + 1) * slots + i
            b_ref[k * slots + i] = (half[i].astype(F32) * before[place].astype(F32)).astype(BF16)
    left_copy.wait()


def ready_left(halves, before, left):
    slots, _, cap, _ = left.shape
    return pl.pallas_call(
        ready_kernel,
        out_shape=[
            jax.ShapeDtypeStruct((3 * slots, cap, cap), BF16),
            pltpu.VMEM(left.shape, BF16),
        ],
        in_specs=[whole()] * 4 + [whole(HBM)],
        out_specs=[whole()] * 2,
        scratch_shapes=[pltpu.SemaphoreType.DMA],
        compiler_params=params(),
        cost_estimate=cost(3 * slots * cap * cap, 2 * left.size),
        name="ready_left",
    )(*halves, before, in_hbm(left))


def copy_kernel(right_hbm, right_ref, sem):
    right_copy = pltpu.make_async_copy(right_hbm, right_ref, sem)
    right_copy.start()
    right_copy.wait()


def ready_right(right):
    return pl.pallas_call(
        copy_kernel,
        out_shape=pltpu.VMEM(right.shape, BF16),
        in_specs=[whole(HBM)],
        out_specs=whole(),
        scratch_shapes=[pltpu.SemaphoreType.DMA],
        compiler_params=params(),
        cost_estimate=cost(right.size, 2 * right.size),
        name="ready_right",
    )(in_hbm(right))


def first_close(plan, psi, ops, env_own, env_got, other_h, other_d, half):
    slots, cap, _ = half.shape
    return pl.pallas_call(
        close_kernel,
        out_shape=[
            jax.ShapeDtypeStruct((slots, cap, cap), BF16),
            jax.ShapeDtypeStruct((slots, cap, cap), F32),
            jax.ShapeDtypeStruct((slots // 2 * cap, cap), BF16),
            jax.ShapeDtypeStruct((slots // 2 * cap + 16, cap), BF16),
        ],
        in_specs=[whole(SMEM)] + [whole()] * 7,
        out_specs=[whole()] * 4,
        scratch_shapes=[
            pltpu.VMEM((slots, cap, cap), F32),
            pltpu.VMEM((cap, slots), F32),
        ],
        compiler_params=params(),
        cost_estimate=cost(2 * slots * cap**3, 20 * slots * cap * cap),
        name="first_close",
    )(plan, psi, ops, env_own, env_got, other_h, other_d, half)


def later_step(plan, entries, a_own, lower, got, far_b, before, env, half, left, right, last):
    slots, terms, cap, _ = left.shape
    rows = slots // 2 * cap
    sent = [jax.ShapeDtypeStruct((16 if last else rows + 16, cap), BF16)]
    if not last:
        sent = [jax.ShapeDtypeStruct((rows, cap), BF16)] + sent
    return pl.pallas_call(
        functools.partial(later_kernel, last, entries),
        out_shape=[
            jax.ShapeDtypeStruct((4 * slots, cap, cap), BF16),
            jax.ShapeDtypeStruct((slots, cap, cap), F32),
            *sent,
        ],
        in_specs=[whole(SMEM)] + [whole()] * 14,
        out_specs=[whole()] * (2 + len(sent)),
        scratch_shapes=[
            pltpu.VMEM((slots, cap, cap), F32),
            pltpu.VMEM((cap, terms * cap), BF16),
        ],
        compiler_params=params(),
        cost_estimate=step_cost(left),
        name="last_step" if last else "later_step",
    )(plan, a_own, lower, *got, far_b, before, env, half, left, right)


def near_kernel(a_ref, psi_ref, half_ref, near_ref):
    for j in range(a_ref.shape[0]):
        near_ref[0, j] = a_ref[j].astype(BF16)
        near_ref[1, j] = (half_ref[j] * psi_ref[j].astype(F32)).astype(BF16)


def near_message(a_own, psi, half):
    slots, cap, _ = a_own.shape
    return pl.pallas_call(
        near_kernel,
        out_shape=jax.ShapeDtypeStruct((2, slots, cap, cap), BF16),
        in_specs=[whole()] * 3,
        out_specs=whole(),
        compiler_params=params(),
        cost_estimate=cost(2 * slots * cap * cap, 12 * slots * cap * cap),
        name="near_message",
    )(a_own, psi, half)


def settle_kernel(entries, tile_0, tile_1, tile_2, tile_3, factors_ref, energy_ref):
    tiles = [t[...] for t in (tile_0, tile_1, tile_2, tile_3)]
    rayleigh, deltas, scale = resolve(tiles, entries)
    energy_ref[0] = rayleigh[0, 0]
    factors_ref[...] = pack_rows([scale, deltas[0]], factors_ref.shape[1])


def settle(tiles, entries):
    cap = tiles[0].shape[1]
    return pl.pallas_call(
        functools.partial(settle_kernel, entries),
        out_shape=[jax.ShapeDtypeStruct((16, cap), BF16), jax.ShapeDtypeStruct((1,), F32)],
        in_specs=[whole()] * 4,
        out_specs=[whole(), whole(SMEM)],
        compiler_params=params(),
        cost_estimate=cost(16 * cap, 128 * cap),
        name="settle",
    )(*tiles)


def ground_kernel(plan, factors_ref, a_ref, psi_ref, half_ref, inv_sv, ground_ref, scaled_ref):
    slots, cap = a_ref.shape[0], a_ref.shape[1]
    scale, delta = unpack_rows(factors_ref[...], 2)
    lane = lax.broadcasted_iota(jnp.int32, (1, cap), 1)
    for j in range(slots):
        b = half_ref[j] * psi_ref[j].astype(F32)
        ground = (scale * (a_ref[j] + delta * b)).astype(BF16)
        ground_ref[j] = ground
        weight = jnp.where(lane < plan[RANKS + j], inv_sv[j : j + 1, :] / cap, 0.0)
        scaled_ref[j] = (ground.astype(F32) * weight).astype(BF16)


def ground_state(plan, factors, a_own, psi, half, inv_sv):
    slots, cap, _ = a_own.shape
    return pl.pallas_call(
        ground_kernel,
        out_shape=[jax.ShapeDtypeStruct((slots, cap, cap), BF16)] * 2,
        in_specs=[whole(SMEM)] + [whole()] * 5,
        out_specs=[whole(), whole()],
        compiler_params=params(),
        cost_estimate=cost(4 * slots * cap * cap, 12 * slots * cap * cap),
        name="ground_state",
    )(plan, factors, a_own, psi, half, inv_sv)


def merge_kernel(factors_ref, scaled_ref, near_ref, out_ref):
    live = lax.axis_index("sect") < lax.axis_size("sect") - 1
    scale, delta = unpack_rows(factors_ref[...], 2)
    for j in range(scaled_ref.shape[0]):
        following = scale * (near_ref[0, j].astype(F32) + delta * near_ref[1, j].astype(F32))
        merged = jnp.dot(scaled_ref[j], following.astype(BF16), preferred_element_type=F32)
        out_ref[j] = jnp.where(live, merged, 0.0).astype(BF16)


def merge(factors, scaled, near):
    slots, cap, _ = scaled.shape
    return pl.pallas_call(
        merge_kernel,
        out_shape=jax.ShapeDtypeStruct((slots, cap, cap), BF16),
        in_specs=[whole()] * 3,
        out_specs=whole(),
        compiler_params=params(),
        cost_estimate=cost(2 * slots * cap**3, 6 * slots * cap * cap),
        name="merge",
    )(factors, scaled, near)


def around(value, shift):
    count = lax.axis_size("blk")
    return lax.ppermute(value, "blk", [(i, (i + shift) % count) for i in range(count)])


def three(value):
    return [around(value, shift) for shift in (1, 2, 3)]


def pass_on(upper, lower, beside):
    upper_1 = around(upper, 1)
    lower_3 = around(lower, 3)
    lower_1 = around(lower, 1)
    upper_3 = around(upper, 3)
    done = list(beside())
    lower_3, done[0] = lax.optimization_barrier((lower_3, done[0]))
    upper_1, upper_3 = lax.optimization_barrier((upper_1, upper_3))
    upper_2 = around(upper_1, 1)
    lower_2 = around(lower_3, 3)
    return [upper_1, lower_1, upper_2, lower_2, upper_3, lower_3], done


def shards(
    psi_guess,
    sector_sizes,
    slot_sector,
    pair_table,
    left_ops,
    right_ops,
    decay,
    source_h,
    precond,
    inv_sv,
    ranks,
):
    sections = lax.axis_size("sect")
    chips = sections // 2
    slots, cap = psi_guess.shape[1], psi_guess.shape[2]
    entries = float(slot_sector.shape[0] * cap * cap)
    left, right = left_ops[0], right_ops[0]

    swap = [(i, i ^ 1) for i in range(sections)]
    other_h = lax.ppermute(source_h[0], "sect", swap)
    other_d = lax.ppermute(decay[0], "sect", swap)
    plan, own_psi, own_h, own_d, near_precond = start(
        slot_sector, pair_table, sector_sizes, ranks, psi_guess[0], source_h[0], decay[0], precond[0]
    )
    maps = chip_maps(own_h, other_h, own_d, other_d, chips)
    groups = [[2 * q + c for q in range(chips)] for c in range(2)]
    got_maps = lax.all_to_all(maps, "sect", 0, 0, tiled=True, axis_index_groups=groups)
    own_psi, late_precond, _ = lax.optimization_barrier((own_psi, near_precond, maps))
    got_psi = three(own_psi)
    own_half, half = half_message(late_precond)
    halves = three(own_half)
    got_maps, own_half = lax.optimization_barrier((got_maps, own_half))
    env = scan_maps(got_maps)
    got_env = lax.all_to_all(env, "sect", 0, 0, tiled=True, axis_index_groups=groups)
    env_own = got_env.reshape(slots // 2, cap, cap)
    psi, ops = first_products(plan, [own_psi] + got_psi, left, right)
    env_own, ops, halves[1:] = lax.optimization_barrier((env_own, ops, halves[1:]))
    env_got = lax.ppermute(env_own, "sect", swap)
    env_low, a_own, upper, lower = first_close(
        plan, psi, ops, env_own, env_got, other_h, other_d, half
    )
    lower, halves[0] = lax.optimization_barrier((lower, halves[0]))
    for step in range(1, STEPS):
        last = step == STEPS - 1
        later_left, later_right, _ = lax.optimization_barrier((left, right, lower))
        got, (far_b, later_left) = pass_on(
            upper, lower, functools.partial(ready_left, halves, psi, later_left)
        )
        later_right = ready_right(later_right)
        psi, a_own, *sent = later_step(
            plan, entries, a_own, lower, got, far_b, psi, env_low, half, later_left, later_right, last
        )
        upper, lower = sent[0], sent[-1]
    tile = lower
    near = near_message(a_own, psi, half)
    behind = [(i + 1, i) for i in range(sections - 1)]
    near = lax.ppermute(near, "sect", behind)
    factors, energies = settle([tile] + three(tile), entries)
    near_factors = lax.ppermute(factors, "sect", behind)
    ground, scaled = ground_state(plan, factors, a_own, psi, half, inv_sv[0])
    merged = merge(near_factors, scaled, near)
    return (ground[None], energies, merged[None])


def solution(mesh):
    in_specs = (
        P("sect", "blk", None, None),
        P("sect", None),
        P(),
        P(),
        P("sect", "blk", None, None, None),
        P("sect", "blk", None, None, None),
        P("sect", "blk", None),
        P("sect", "blk", None, None),
        P("sect", "blk", None, None),
        P("sect", "blk", None),
        P("sect", None),
    )
    out_specs = (P("sect", "blk", None, None), P("sect"), P("sect", "blk", None, None))
    return jax.shard_map(shards, mesh=mesh, in_specs=in_specs, out_specs=out_specs, check_vma=False)
```
